32 devices in a mesh: groups: 2 (over y), leaf: 8 (over z, x), sub: 2 (over core).
Axes of the slice: x: 2, y: 2, z: 4, core: 2. Of those that a mesh axis runs over, the one named last changes fastest.
Arguments:
- vectors: float32 [32, 32768], P('sub', ('groups', 'leaf')), parts along dimension 1, may hold values from -6 to 6
- points: float32 [3, 32768], P(None, ('groups', 'leaf')), parts along dimension 1, may hold values from 0 to 1
- leaf_basis: float32 [256, 64, 128], P(('groups', 'leaf')), parts along dimension 0, may hold values from -0.5 to 0.5
- local_transfer: float32 [496, 64, 64], P(('groups', 'leaf')), parts along dimension 0, may hold values from -0.5 to 0.5
- local_skeleton: float32 [480, 3, 64], P(('groups', 'leaf')), parts along dimension 0, may hold values from 0 to 1
- upper_transfer: float32 [6, 64, 64], replicated, may hold values from -0.5 to 0.5
- upper_skeleton: float32 [15, 3, 64], replicated, may hold values from 0 to 1
- near_list: int32 [2, 8192], P(None, ('groups', 'leaf')), parts along dimension 1, may hold values from 0 to 47, as said below
- far_list: int32 [2, 2048], P(None, ('groups', 'leaf')), parts along dimension 1, may hold values from 0 to 89, as said below
- upper_list: int32 [2, 256], P(None, ('groups', 'leaf')), parts along dimension 1, may hold values from 0 to 13, as said below
Outputs:
- product: float32 [32, 32768], P('sub', ('groups', 'leaf')), parts along dimension 1
The draws below stay inside these ranges and needn't reach their ends.
There are 2 independent parts, one for each index of `groups`. The reference program is written for one: setup_inputs(seed, part) draws one part's arguments, and reference() takes and returns one part's arrays. A program takes and returns all parts, laid end to end along the dimension named above; an argument that names none is the same for every part. Nothing has to cross between parts.
Inputs may be any that keep to these rules, and one draw needn't show every extreme that they name: near_list[0] is a leaf of the owner, 0 to 15; near_list[1] counts leaves from the first leaf of the previous owner, 0 to 47. far_list[0] is a node of the owner below its root; far_list[1] counts nodes below the roots of owners o - 1, o, o + 1 in a row, and names a node of the same level as the row node. `upper_list`: both nodes of a pair are of the same level, never the root; an owner's pairs may name any upper nodes.
All inputs are finite; a program needn't handle non-finite values.
Results may differ from the reference program's by a relative error of at most 0.0003.
Values sent between devices are 32-bit elements; how exact they have to be, the bound alone decides.
A program may use at most 128 MiB of HBM per device.

```python
import math
from functools import partial
import jax
import jax.numpy as jnp
import numpy as np
from jax import lax

LEAF = 128
RANK = 64
NV = 32
LPD = 16
NEAR_CAP = 512
FAR_CAP = 128
UP_PAIRS = 128
LEAVES = 128
NPTS = 16384
NEAR_ALL = 4096
N_LEAF = 8


def level_lookup(count, nodes):
    anchors = []
    extents = []
    anchor = 0
    extent = count
    while extent >= 1:
        anchors += [anchor] * extent
        extents += [extent] * extent
        anchor += extent
        extent //= 2
    return (jnp.asarray(np.array(anchors[:nodes], np.int32)), jnp.asarray(np.array(extents[:nodes], np.int32)))


def draw_near_list(key, part):
    key = jax.random.fold_in(key, 5)
    first_key, second_key = jax.random.split(key)
    total = NEAR_CAP * N_LEAF
    row_ids = jax.random.randint(first_key, (total,), 0, LPD)
    col_ids = jax.random.randint(second_key, (total,), 0, 3 * LPD)
    col_ids = col_ids.at[0].set(3 * LPD - 1).at[1].set(0)
    return jnp.stack([row_ids, col_ids]).astype(jnp.int32)


def draw_far_list(key, part):
    key = jax.random.fold_in(key, 7)
    first_key, second_key, third_key = jax.random.split(key, 3)
    total = FAR_CAP * N_LEAF
    lower_count = 2 * LPD - 2
    anchors, extents = level_lookup(LPD, lower_count)
    row_ids = jax.random.randint(first_key, (total,), 0, lower_count)
    row_ids = row_ids.at[0].set(lower_count - 1).at[1].set(0)
    neighbour = jax.random.randint(second_key, (total,), 0, 3).at[0].set(2).at[1].set(0)
    within = jax.random.randint(third_key, (total,), 0, LPD) % extents[row_ids]
    within = within.at[0].set(1).at[1].set(0)
    col_ids = neighbour * lower_count + anchors[row_ids] + within
    return jnp.stack([row_ids, col_ids]).astype(jnp.int32)


def draw_upper_list(key, part):
    key = jax.random.fold_in(key, 9)
    first_key, second_key = jax.random.split(key)
    nodes = 2 * N_LEAF - 2
    anchors, extents = level_lookup(N_LEAF, nodes)
    row_ids = jax.random.randint(first_key, (UP_PAIRS,), 0, nodes)
    row_ids = row_ids.at[0].set(nodes - 1).at[1].set(0)
    within = jax.random.randint(second_key, (UP_PAIRS,), 0, N_LEAF) % extents[row_ids]
    within = within.at[0].set(1).at[1].set(0)
    col_ids = anchors[row_ids] + within
    return jnp.stack([row_ids, col_ids]).astype(jnp.int32)


def shard_levels(key, shape, cuts, least, top_value):
    def one(axis_at, blocks):
        heights = jax.random.uniform(jax.random.fold_in(jax.random.fold_in(key, 6), axis_at), (blocks,), jnp.float32, least / len(cuts), top_value / len(cuts))
        return jnp.repeat(jnp.exp(heights), shape[axis_at] // blocks).reshape((-1,) + (1,) * (len(shape) - axis_at - 1))

    gain = one(*cuts[0])
    for cut in cuts[1:]:
        gain = gain * one(*cut)
    return gain


def gaussian(own_key, dims, scale, most, pieces=(), held_as=jnp.bfloat16):
    values = scale * jax.random.normal(own_key, dims, jnp.float32)
    if pieces:
        values = values * shard_levels(own_key, dims, pieces, -0.22, 0.18)
    return jnp.clip(values, -most, most).astype(held_as)


def setup_inputs(seed: int = 0, part: int = 0) -> dict:
    key_of = jax.random.split(jax.random.key(seed), 11)
    part_keys = jax.random.split(jax.random.fold_in(key_of[10], part), 11)
    vectors = gaussian(part_keys[0], (NV, NPTS), 1.0, 6.0, ((0, 2), (1, 8)), jnp.float32)
    points = jnp.clip(1.0 * jax.random.uniform(part_keys[1], (3, NPTS), jnp.float32) ** shard_levels(part_keys[1], (3, NPTS), ((1, 8),), -0.2, 0.2), 0.0, 1.0)
    leaf_basis = gaussian(part_keys[2], (LEAVES, RANK, LEAF), LEAF ** -0.5, 0.5, ((0, 8),), jnp.float32)
    local_transfer = gaussian(part_keys[3], (N_LEAF * (2 * LPD - 1), RANK, RANK), (2 * RANK) ** -0.5, 0.5, ((0, 8),), jnp.float32)
    local_skeleton = jnp.clip(1.0 * jax.random.uniform(part_keys[4], (N_LEAF * (2 * LPD - 2), 3, RANK), jnp.float32) ** shard_levels(part_keys[4], (N_LEAF * (2 * LPD - 2), 3, RANK), ((0, 8),), -0.2, 0.2), 0.0, 1.0)
    upper_transfer = gaussian(key_of[5], (N_LEAF - 2, RANK, RANK), (2 * RANK) ** -0.5, 0.5, (), jnp.float32)
    upper_skeleton = jnp.clip(jax.random.uniform(key_of[6], (2 * N_LEAF - 1, 3, RANK), jnp.float32, 0.0, 1.0), 0.0, 1.0)
    near_list = draw_near_list(jax.random.fold_in(jax.random.fold_in(key_of[10], part), 71), part)
    far_list = draw_far_list(jax.random.fold_in(jax.random.fold_in(key_of[10], part), 71), part)
    upper_list = draw_upper_list(jax.random.fold_in(jax.random.fold_in(key_of[10], part), 71), part)
    return {"vectors": vectors, "points": points, "leaf_basis": leaf_basis, "local_transfer": local_transfer, "local_skeleton": local_skeleton, "upper_transfer": upper_transfer, "upper_skeleton": upper_skeleton, "near_list": near_list, "far_list": far_list, "upper_list": upper_list}


root_three = math.sqrt(3.0)
length_scale = 0.3
highest = lax.Precision.HIGHEST

def matern(targets, sources):
    separation = targets[..., :, :, None] - sources[..., :, None, :]
    scaled = jnp.sqrt(lax.optimization_barrier(jnp.sum(separation * separation, axis=-3))) * (root_three / length_scale)
    return (1.0 + scaled) * jnp.exp(-scaled)

def level_table(count):
    offsets = []
    counts = []
    anchor = 0
    extent = count
    while extent >= 1:
        offsets.append(anchor)
        counts.append(extent)
        anchor += extent
        extent //= 2
    return (offsets, counts)

def pair_sum(values):
    return values.reshape((values.shape[0] // 2, 2) + values.shape[1:]).sum(axis=1)

def upsweep(leaf_coefs, transfer, offsets, counts):
    levels = [leaf_coefs]
    for height in range(len(counts) - 1):
        anchor = offsets[height]
        extent = counts[height]
        lifted = jnp.einsum('nab,nvb->nva', transfer[anchor:anchor + extent], levels[-1], precision=highest)
        levels.append(pair_sum(lifted))
    return jnp.concatenate(levels, axis=0)

def downsweep(node_y, transfer, offsets, counts):
    for height in range(len(counts) - 2, -1, -1):
        anchor = offsets[height]
        extent = counts[height]
        above = offsets[height + 1]
        parents = jnp.repeat(node_y[above:above + counts[height + 1]], 2, axis=0)
        lowered = jnp.einsum('nab,nva->nvb', transfer[anchor:anchor + extent], parents, precision=highest)
        node_y = node_y.at[anchor:anchor + extent].add(lowered)
    return node_y

def upper_build(root_coefs, root_lifted, upper_transfer, n_leaf):
    offsets, counts = level_table(n_leaf)
    levels = [root_coefs, pair_sum(root_lifted)]
    for height in range(1, len(counts) - 1):
        anchor = offsets[height] - n_leaf
        lifted = jnp.einsum('nab,nvb->nva', upper_transfer[anchor:anchor + counts[height]], levels[-1], precision=highest)
        levels.append(pair_sum(lifted))
    return jnp.concatenate(levels, axis=0)

def upper_down(upper_y, upper_transfer, n_leaf):
    offsets, counts = level_table(n_leaf)
    for height in range(len(counts) - 2, 0, -1):
        anchor = offsets[height]
        extent = counts[height]
        above = offsets[height + 1]
        parents = jnp.repeat(upper_y[above:above + counts[height + 1]], 2, axis=0)
        lowered = jnp.einsum('nab,nva->nvb', upper_transfer[anchor - n_leaf:anchor - n_leaf + extent], parents, precision=highest)
        upper_y = upper_y.at[anchor:anchor + extent].add(lowered)
    return upper_y

def couple(row_skeleton, col_skeleton, col_coefs, row_ids, col_ids, count):
    block_size = math.gcd(row_ids.shape[0], 256)

    def add_block(running, indices):
        row_block, col_block = indices
        kernel = matern(row_skeleton[row_block], col_skeleton[col_block])
        products = jnp.einsum('gab,gvb->gva', kernel, col_coefs[col_block], precision=highest)
        return (running.at[row_block].add(products), None)
    start_value = jnp.zeros((count,) + col_coefs.shape[1:], jnp.float32)
    result, _ = lax.scan(add_block, start_value, (row_ids.reshape(-1, block_size), col_ids.reshape(-1, block_size)))
    return result

def reference(vectors, points, leaf_basis, local_transfer, local_skeleton, upper_transfer, upper_skeleton, near_list, far_list, upper_list):
    leaves_all = N_LEAF * LPD
    lower_count = 2 * LPD - 2
    x_leaves = vectors.reshape(NV, leaves_all, LEAF)
    leaf_points = points.reshape(3, leaves_all, LEAF)
    padding = ((0, 0), (LPD, LPD), (0, 0))
    x_padded = jnp.pad(x_leaves, padding)
    points_padded = jnp.pad(leaf_points, padding)
    owner_base = (jnp.arange(N_LEAF, dtype=jnp.int32) * LPD)[:, None]
    near_rows = (near_list[0].reshape(N_LEAF, NEAR_CAP) + owner_base).reshape(-1)
    near_cols = (near_list[1].reshape(N_LEAF, NEAR_CAP) + owner_base).reshape(-1)
    block_size = math.gcd(NEAR_ALL, 64)

    def near_block(running, indices):
        row_block, col_block = indices
        kernel = matern(jnp.transpose(leaf_points[:, row_block], (1, 0, 2)), jnp.transpose(points_padded[:, col_block], (1, 0, 2)))
        products = jnp.einsum('gij,vgj->vgi', kernel, x_padded[:, col_block], precision=highest)
        return (running.at[:, row_block].add(products), None)
    near_part, _ = lax.scan(near_block, jnp.zeros((NV, leaves_all, LEAF), jnp.float32), (near_rows.reshape(-1, block_size), near_cols.reshape(-1, block_size)))
    offsets, counts = level_table(LPD)
    leaf_coefs = jnp.einsum('nri,vni->nvr', leaf_basis, x_leaves, precision=highest).reshape(N_LEAF, LPD, NV, RANK)
    transfers = local_transfer.reshape(N_LEAF, 2 * LPD - 1, RANK, RANK)
    coefs = jax.vmap(partial(upsweep, offsets=offsets, counts=counts))(leaf_coefs, transfers)
    lower_padded = jnp.pad(coefs[:, :lower_count], ((1, 1), (0, 0), (0, 0), (0, 0))).reshape(-1, NV, RANK)
    skeleton_padded = jnp.pad(local_skeleton.reshape(N_LEAF, lower_count, 3, RANK), ((1, 1), (0, 0), (0, 0), (0, 0))).reshape(-1, 3, RANK)
    lower_base = (jnp.arange(N_LEAF, dtype=jnp.int32) * lower_count)[:, None]
    far_rows = (far_list[0].reshape(N_LEAF, FAR_CAP) + lower_base).reshape(-1)
    far_cols = (far_list[1].reshape(N_LEAF, FAR_CAP) + lower_base).reshape(-1)
    lower_y = couple(local_skeleton, skeleton_padded, lower_padded, far_rows, far_cols, N_LEAF * lower_count)
    root_coefs = coefs[:, lower_count]
    root_lifted = jnp.einsum('nab,nvb->nva', transfers[:, lower_count], root_coefs, precision=highest)
    upper_coefs = upper_build(root_coefs, root_lifted, upper_transfer, N_LEAF)
    upper_y = couple(upper_skeleton, upper_skeleton, upper_coefs, upper_list[0], upper_list[1], 2 * N_LEAF - 1)
    upper_y = upper_down(upper_y, upper_transfer, N_LEAF)
    parent_y = jnp.repeat(upper_y[N_LEAF:N_LEAF + N_LEAF // 2], 2, axis=0)
    root_y = upper_y[:N_LEAF] + jnp.einsum('nab,nva->nvb', transfers[:, lower_count], parent_y, precision=highest)
    node_y = jnp.concatenate([lower_y.reshape(N_LEAF, lower_count, NV, RANK), root_y[:, None]], axis=1)
    node_y = jax.vmap(partial(downsweep, offsets=offsets, counts=counts))(node_y, transfers)
    far_part = jnp.einsum('nri,nvr->vni', leaf_basis, node_y[:, :LPD].reshape(leaves_all, NV, RANK), precision=highest)
    return (near_part + far_part).reshape(NV, leaves_all * LEAF)
```

```python
import functools
import math

import jax
import jax.numpy as jnp
from jax import lax
from jax.experimental import pallas as pl
from jax.experimental.pallas import tpu as pltpu
from jax.sharding import PartitionSpec as P

root_three = math.sqrt(3.0)
length_scale = 0.3
log2e = math.log2(math.e)
ln2 = math.log(2.0)
point_scale = root_three / length_scale * log2e
highest = lax.Precision.HIGHEST
MESH = pl.DeviceIdType.MESH
FEATURES = 32
GROUP = 4
f32 = jnp.float32
bf16 = jnp.bfloat16


def level_table(count):
    offsets = []
    counts = []
    anchor = 0
    extent = count
    while extent >= 1:
        offsets.append(anchor)
        counts.append(extent)
        anchor += extent
        extent //= 2
    return (offsets, counts)


def dot_nt(a, b):
    return lax.dot_general(
        a, b, (((1,), (1,)), ((), ())), precision=highest, preferred_element_type=f32
    )


def dot_nn(a, b):
    return lax.dot_general(
        a, b, (((1,), (0,)), ((), ())), precision=highest, preferred_element_type=f32
    )


def dot_fast(a, b):
    return lax.dot_general(a, b, (((1,), (0,)), ((), ())), preferred_element_type=f32)


def each(start, stop, body):
    if stop - start <= 16:
        for i in range(start, stop):
            body(i)
    else:

        @pl.loop(start, stop)
        def _(i):
            body(i)


def exchange_kernel(
    n,
    halo_width,
    x_ref,
    pts_ref,
    basis_ref,
    tr_ref,
    ulist_ref,
    nlist_ref,
    xall,
    ptsall,
    call,
    roots,
    cols_out,
    wts_out,
    halo_send,
    halo_recv,
    root_send,
    root_recv,
):
    me = lax.axis_index("leaf")
    leaf_count, rank, leaf = basis_ref.shape
    vecs = x_ref.shape[0]
    lower = 2 * leaf_count - 2
    offsets, counts = level_table(leaf_count)
    entries = ulist_ref.shape[1]

    barrier = pltpu.get_barrier_semaphore()

    def greet(d):
        pl.semaphore_signal(
            barrier, inc=1, device_id={"leaf": lax.rem(me + d, n)}, device_id_type=MESH
        )

    each(1, n, greet)
    pl.semaphore_wait(barrier, n - 1)

    own_pts = pts_ref.at[:, pl.ds(0, halo_width)]
    own_coefs = call.at[pl.ds(lower, lower)]
    sources = (x_ref, own_pts, own_coefs)

    def halo(kind, side):
        slot = 2 * side
        target = (xall.at[slot], ptsall.at[slot], call.at[pl.ds(slot * lower, lower)])[kind]
        other = jnp.minimum(me + 1, n - 1) if side == 0 else jnp.maximum(me - 1, 0)
        return pltpu.make_async_remote_copy(
            src_ref=sources[kind],
            dst_ref=target,
            send_sem=halo_send.at[kind, side],
            recv_sem=halo_recv.at[kind, side],
            device_id={"leaf": other},
            device_id_type=MESH,
        )

    def sends(side):
        return me < n - 1 if side == 0 else me > 0

    def receives(side):
        return me > 0 if side == 0 else me < n - 1

    for side in range(2):

        @pl.when(sends(side))
        def _():
            halo(0, side).start()
            halo(1, side).start()

    def up(node):
        return dot_nt(call[lower + node], tr_ref[node])

    for i in range(leaf_count):
        call[lower + i] = dot_nt(x_ref[:, i * leaf : (i + 1) * leaf], basis_ref[i])
    for height in range(1, len(counts) - 1):
        below = offsets[height - 1]
        for j in range(counts[height]):
            call[lower + offsets[height] + j] = up(below + 2 * j) + up(below + 2 * j + 1)
    for side in range(2):

        @pl.when(sends(side))
        def _():
            halo(2, side).start()

    root = up(lower - 2) + up(lower - 1)
    roots[me] = jnp.zeros(roots.shape[1:], f32)
    roots[me, 0:vecs, 0:rank] = root
    roots[me, 0:vecs, rank : 2 * rank] = dot_nt(root, tr_ref[lower])
    roots[me, vecs : vecs + 2, 0:entries] = ulist_ref[...].astype(f32)

    def root_copy(d):
        return pltpu.make_async_remote_copy(
            src_ref=roots.at[me],
            dst_ref=roots.at[me],
            send_sem=root_send.at[d],
            recv_sem=root_recv.at[d],
            device_id={"leaf": lax.rem(me + d, n)},
            device_id_type=MESH,
        )

    def root_arrival(d):
        sender = lax.rem(me + n - d, n)
        return pltpu.make_async_remote_copy(
            src_ref=roots.at[me],
            dst_ref=roots.at[sender],
            send_sem=root_send.at[d],
            recv_sem=root_recv.at[d],
            device_id={"leaf": lax.rem(me + d, n)},
            device_id_type=MESH,
        )

    each(1, n, lambda d: root_copy(d).start())

    xall[1] = x_ref[...]
    ptsall[1] = pts_ref[:, 0:halo_width]
    for side in range(2):
        slot = 2 * side

        @pl.when(jnp.logical_not(receives(side)))
        def _():
            xall[slot] = jnp.zeros(xall.shape[1:], f32)
            ptsall[slot] = jnp.zeros(ptsall.shape[1:], f32)
            call[slot * lower : (slot + 1) * lower] = jnp.zeros((lower,) + call.shape[1:], f32)

    total = nlist_ref.shape[1]
    row_hot = (
        lax.broadcasted_iota(jnp.int32, (leaf_count, total), 0) == nlist_ref[0:1, :]
    ).astype(f32).astype(bf16)
    col_hot = (
        lax.broadcasted_iota(jnp.int32, (128, total), 0) == nlist_ref[1:2, :]
    ).astype(f32).astype(bf16)
    count = lax.dot_general(
        row_hot, col_hot, (((1,), (1,)), ((), ())), preferred_element_type=f32
    )
    has = (count > 0.5).astype(f32)
    before = (
        lax.broadcasted_iota(jnp.int32, (128, 128), 0)
        < lax.broadcasted_iota(jnp.int32, (128, 128), 1)
    ).astype(f32).astype(bf16)
    place = dot_fast(has.astype(bf16), before)
    place = jnp.where(has > 0.5, place, -1.0)
    lane = lax.broadcasted_iota(jnp.int32, (leaf_count, 128), 1)
    lane_f = lane.astype(f32)
    cols = jnp.zeros((leaf_count, 128), f32)
    wts = jnp.zeros((leaf_count, 128), f32)
    for c in range(3 * leaf_count):
        hit = place[:, c : c + 1] == lane_f
        cols = cols + jnp.where(hit, float(c), 0.0)
        wts = wts + jnp.where(hit, count[:, c : c + 1], 0.0)
    filled = jnp.sum(has, axis=1, keepdims=True)
    cols_out[...] = jnp.where(lane == 127, filled, cols).astype(jnp.int32)
    wts_out[...] = wts * ln2

    for side in range(2):

        @pl.when(sends(side))
        def _():
            for kind in range(3):
                halo(kind, side).wait_send()

        @pl.when(receives(side))
        def _():
            for kind in range(3):
                halo(kind, side).wait_recv()

    def finish(d):
        root_copy(d).wait_send()
        root_arrival(d).wait_recv()

    each(1, n, finish)


def split(values):
    high = values.astype(bf16)
    return high, (values - high.astype(f32)).astype(bf16)


def kernel_values(squared):
    squared = jnp.maximum(squared, 1e-20)
    t = squared * lax.rsqrt(squared)
    return (t + log2e) * jnp.exp2(-t)


def product(values, kernel):
    kernel_high, kernel_low = split(kernel)
    high, low = split(values)
    rows = values.shape[0]
    both = dot_fast(jnp.concatenate([high, low], axis=0), kernel_high)
    return both[:rows] + both[rows:] + dot_fast(high, kernel_low)


def couple_kernel(
    n,
    entries,
    cols_ref,
    wts_ref,
    far_ref,
    xall,
    ptsall,
    uppts_ref,
    call,
    roots,
    basis_ref,
    tr_ref,
    uptr_ref,
    out_ref,
    feat,
    near_t,
    near_row,
    skel_t,
    skel_row,
    up_t,
    up_row,
    y_ref,
    upc,
):
    me = lax.axis_index("leaf")
    leaf_count, rank, leaf = basis_ref.shape
    vecs = out_ref.shape[0]
    lower = 2 * leaf_count - 2
    npts = leaf_count * leaf
    nskel = lower * rank
    offsets, counts = level_table(leaf_count)
    up_offsets, up_counts = level_table(n)

    def features(p):
        q = (p - 0.5) * point_scale
        high = q.astype(bf16).astype(f32)
        low = (q - high).astype(bf16).astype(f32)
        q = high + low
        norm = jnp.sum(q * q, axis=0, keepdims=True)
        n1 = norm.astype(bf16).astype(f32)
        n2 = (norm - n1).astype(bf16).astype(f32)
        n3 = norm - n1 - n2
        return high, low, n1, n2, n3

    def put(p, width):
        high, low, n1, n2, n3 = features(p)
        span = slice(0, width)
        one = jnp.ones((1, width), f32)
        for k, rows in enumerate((high, low, high, low)):
            feat[0, 3 * k : 3 * k + 3, span] = -2.0 * rows
        for k, rows in enumerate((high, high, low, low)):
            feat[1, 3 * k : 3 * k + 3, span] = rows
        for k, rows in enumerate((n1, n2, n3, one, one, one)):
            feat[0, 12 + k : 13 + k, span] = rows
        for k, rows in enumerate((one, one, one, n1, n2, n3)):
            feat[1, 12 + k : 13 + k, span] = rows

    def columns_to(target, first, start, width):
        for t in range(width // 128):
            tile = feat[0, :, start + t * 128 : start + (t + 1) * 128]
            target[first + t * 128 : first + (t + 1) * 128, :] = tile.T.astype(bf16)

    def rows_to(target, start, nodes):
        for j in range(nodes):
            target[j] = feat[1, :, start + j * rank : start + (j + 1) * rank].astype(bf16)

    feat[...] = jnp.zeros(feat.shape, f32)
    for slot in range(3):
        put(ptsall[slot], npts + nskel)
        columns_to(near_t, slot * npts, 0, npts)
        columns_to(skel_t, slot * nskel, npts, nskel)
        if slot == 1:
            near_row[...] = feat[1, :, 0:npts].astype(bf16)
            rows_to(skel_row, npts, lower)

    chunk = math.gcd(uppts_ref.shape[1], 1024)

    def up_chunk(i):
        base = i * chunk if isinstance(i, int) else pl.multiple_of(i * chunk, chunk)
        put(uppts_ref[:, pl.ds(base, chunk)], chunk)
        for t in range(chunk // 128):
            tile = feat[0, :, t * 128 : (t + 1) * 128]
            up_t[pl.ds(base + t * 128, 128), :] = tile.T.astype(bf16)
        for j in range(chunk // rank):
            up_row[i * (chunk // rank) + j] = feat[1, :, j * rank : (j + 1) * rank].astype(bf16)

    each(0, uppts_ref.shape[1] // chunk, up_chunk)

    def load_roots(j):
        upc[j] = roots[j, 0:vecs, 0:rank]

    each(0, n, load_roots)

    def first_lift(j):
        upc[n + j] = roots[2 * j, 0:vecs, rank : 2 * rank] + roots[2 * j + 1, 0:vecs, rank : 2 * rank]

    each(0, n // 2, first_lift)
    for height in range(2, len(up_counts)):

        def lift(j, height=height):
            child = up_offsets[height - 1] + 2 * j
            upc[up_offsets[height] + j] = dot_nt(upc[child], uptr_ref[child - n]) + dot_nt(
                upc[child + 1], uptr_ref[child + 1 - n]
            )

        each(0, up_counts[height], lift)

    pair_rows = roots[:, vecs, :]
    pair_cols = roots[:, vecs + 1, :]
    used = lax.broadcasted_iota(jnp.int32, pair_rows.shape, 1) < entries
    value = None
    for height in range(len(up_counts) - 1, -1, -1):
        node = up_offsets[height] + lax.div(me, 2**height)
        mine = jnp.logical_and(pair_rows == node.astype(f32), used)
        row_feat = up_row[node]

        def term(c, mine=mine, row_feat=row_feat):
            named = jnp.logical_and(mine, pair_cols == jnp.asarray(c, f32))
            times = jnp.sum(jnp.sum(jnp.where(named, ln2, 0.0), axis=1, keepdims=True), axis=0, keepdims=True)
            start = c * rank if isinstance(c, int) else pl.multiple_of(c * rank, rank)
            kernel = kernel_values(dot_fast(up_t[pl.ds(start, rank), :], row_feat))
            return product(upc[c] * times, kernel)

        first = up_offsets[height]
        if up_counts[height] <= 16:
            level = sum(term(first + j) for j in range(up_counts[height]))
        else:
            level = lax.fori_loop(
                0,
                up_counts[height],
                lambda j, acc: acc + term(first + j),
                jnp.zeros((vecs, rank), f32),
            )
        if value is not None:
            if height == 0:
                level = level + dot_nn(value, tr_ref[lower])
            else:
                level = level + dot_nn(value, uptr_ref[node - n])
        value = level

    y_ref[...] = jnp.zeros(y_ref.shape, f32)
    y_ref[lower] = value * (1.0 / ln2)

    far_total = far_ref.shape[1]
    far_group = math.gcd(far_total, 4)

    @pl.loop(0, far_total // far_group)
    def _(g):
        done = []
        for k in range(far_group):
            r = far_ref[0, g * far_group + k]
            c = far_ref[1, g * far_group + k]
            squared = dot_fast(skel_t[pl.ds(pl.multiple_of(c * rank, rank), rank), :], skel_row[r])
            done.append((r, product(call[c], kernel_values(squared))))
        for r, part in done:
            y_ref[r] += part

    for height in range(len(counts) - 2, -1, -1):
        for j in range(counts[height]):
            node = offsets[height] + j
            y_ref[node] += dot_nn(y_ref[offsets[height + 1] + j // 2], tr_ref[node])

    @pl.loop(0, leaf_count)
    def _(r):
        lanes = pl.ds(pl.multiple_of(r * leaf, leaf), leaf)
        row_feat = near_row[:, lanes]
        groups = lax.div(cols_ref[r, 127] + (GROUP - 1), GROUP)

        def near_group(g, acc):
            values = []
            places = []
            for k in range(GROUP):
                c = cols_ref[r, g * GROUP + k]
                slot = lax.div(c, leaf_count)
                inside = pl.multiple_of((c - slot * leaf_count) * leaf, leaf)
                values.append(xall[slot, :, pl.ds(inside, leaf)] * wts_ref[r, g * GROUP + k])
                places.append(near_t[pl.ds(pl.multiple_of(c * leaf, leaf), leaf), :])
            kernel = kernel_values(dot_fast(jnp.concatenate(places, axis=0), row_feat))
            return acc + product(jnp.concatenate(values, axis=1), kernel)

        acc = lax.fori_loop(0, groups, near_group, jnp.zeros((vecs, leaf), f32))
        out_ref[:, lanes] = acc + dot_nn(y_ref[r] * ln2, basis_ref[r])


def per_device(
    vectors,
    points,
    leaf_basis,
    local_transfer,
    local_skeleton,
    upper_transfer,
    upper_skeleton,
    near_list,
    far_list,
    upper_list,
):
    leaf_count, rank, leaf = leaf_basis.shape
    vecs, npts = vectors.shape
    n = lax.axis_size("leaf")
    lower = 2 * leaf_count - 2
    nskel = lower * rank
    halo_width = npts + nskel
    nup = 2 * n * rank
    vmem = pl.BlockSpec(memory_space=pltpu.VMEM)
    smem = pl.BlockSpec(memory_space=pltpu.SMEM)
    pts = jnp.concatenate(
        [points, jnp.transpose(local_skeleton, (1, 0, 2)).reshape(3, nskel)], axis=1
    )
    uppts = jnp.pad(
        jnp.transpose(upper_skeleton, (1, 0, 2)).reshape(3, (2 * n - 1) * rank), ((0, 0), (0, rank))
    )
    root_rows = vecs + 8
    xall, ptsall, call, roots, cols, wts = pl.pallas_call(
        functools.partial(exchange_kernel, n, halo_width),
        out_shape=(
            jax.ShapeDtypeStruct((3, vecs, npts), f32),
            jax.ShapeDtypeStruct((3, 3, halo_width), f32),
            jax.ShapeDtypeStruct((3 * lower, vecs, rank), f32),
            jax.ShapeDtypeStruct((n, root_rows, 2 * rank), f32),
            jax.ShapeDtypeStruct((leaf_count, 128), jnp.int32),
            jax.ShapeDtypeStruct((leaf_count, 128), f32),
        ),
        in_specs=[vmem] * 6,
        out_specs=(vmem,) * 6,
        scratch_shapes=[
            pltpu.SemaphoreType.DMA((3, 2)),
            pltpu.SemaphoreType.DMA((3, 2)),
            pltpu.SemaphoreType.DMA((n,)),
            pltpu.SemaphoreType.DMA((n,)),
        ],
        compiler_params=pltpu.CompilerParams(
            collective_id=0, has_side_effects=True, vmem_limit_bytes=40 * 2**20
        ),
    )(vectors, pts, leaf_basis, local_transfer, upper_list, near_list)
    return pl.pallas_call(
        functools.partial(couple_kernel, n, upper_list.shape[1]),
        out_shape=jax.ShapeDtypeStruct((vecs, npts), f32),
        in_specs=[smem] * 3 + [vmem] * 8,
        out_specs=vmem,
        scratch_shapes=[
            pltpu.VMEM((2, FEATURES, halo_width), f32),
            pltpu.VMEM((3 * npts, FEATURES), bf16),
            pltpu.VMEM((FEATURES, npts), bf16),
            pltpu.VMEM((3 * nskel, FEATURES), bf16),
            pltpu.VMEM((lower, FEATURES, rank), bf16),
            pltpu.VMEM((nup, FEATURES), bf16),
            pltpu.VMEM((2 * n, FEATURES, rank), bf16),
            pltpu.VMEM((lower + 1, vecs, rank), f32),
            pltpu.VMEM((2 * n, vecs, rank), f32),
        ],
        compiler_params=pltpu.CompilerParams(vmem_limit_bytes=48 * 2**20),
    )(cols, wts, far_list, xall, ptsall, uppts, call, roots, leaf_basis, local_transfer, upper_transfer)


def solution(mesh):
    return jax.shard_map(
        per_device,
        mesh=mesh,
        in_specs=(
            P("sub", ("groups", "leaf")),
            P(None, ("groups", "leaf")),
            P(("groups", "leaf"), None, None),
            P(("groups", "leaf"), None, None),
            P(("groups", "leaf"), None, None),
            P(),
            P(),
            P(None, ("groups", "leaf")),
            P(None, ("groups", "leaf")),
            P(None, ("groups", "leaf")),
        ),
        out_specs=P("sub", ("groups", "leaf")),
        check_vma=False,
    )
```

```python
import functools
import math

import jax
import jax.numpy as jnp
from jax import lax
from jax.experimental import pallas as pl
from jax.experimental.pallas import tpu as pltpu
from jax.sharding import PartitionSpec as P

root_three = math.sqrt(3.0)
length_scale = 0.3
log2e = math.log2(math.e)
ln2 = math.log(2.0)
point_scale = root_three / length_scale * log2e
highest = lax.Precision.HIGHEST
MESH = pl.DeviceIdType.MESH
FEATURES = 32
GROUP = 16
FAR_GROUP = 16
f32 = jnp.float32
bf16 = jnp.bfloat16


def level_table(count):
    offsets = []
    counts = []
    anchor = 0
    extent = count
    while extent >= 1:
        offsets.append(anchor)
        counts.append(extent)
        anchor += extent
        extent //= 2
    return (offsets, counts)


def dot_nt(a, b):
    return lax.dot_general(
        a, b, (((1,), (1,)), ((), ())), precision=highest, preferred_element_type=f32
    )


def dot_nn(a, b):
    return lax.dot_general(
        a, b, (((1,), (0,)), ((), ())), precision=highest, preferred_element_type=f32
    )


def dot_fast(a, b):
    return lax.dot_general(a, b, (((1,), (0,)), ((), ())), preferred_element_type=f32)


def each(start, stop, body):
    if stop - start <= 16:
        for i in range(start, stop):
            body(i)
    else:

        @pl.loop(start, stop)
        def _(i):
            body(i)


def exchange_kernel(
    n,
    halo_width,
    x_ref,
    pts_ref,
    basis_ref,
    tr_ref,
    ulist_ref,
    nlist_ref,
    xall,
    ptsall,
    packed,
    roots,
    cols_out,
    wts_out,
    halo_send,
    halo_recv,
    root_send,
    root_recv,
    call,
):
    me = lax.axis_index("leaf")
    leaf_count, rank, leaf = basis_ref.shape
    vecs = x_ref.shape[0]
    lower = 2 * leaf_count - 2
    offsets, counts = level_table(leaf_count)
    entries = ulist_ref.shape[1]

    barrier = pltpu.get_barrier_semaphore()

    def greet(d):
        pl.semaphore_signal(
            barrier, inc=1, device_id={"leaf": lax.rem(me + d, n)}, device_id_type=MESH
        )

    each(1, n, greet)
    pl.semaphore_wait(barrier, n - 1)

    own_pts = pts_ref.at[:, pl.ds(0, halo_width)]
    own_coefs = packed.at[1]
    sources = (x_ref, own_pts, own_coefs)

    def halo(kind, side):
        slot = 2 * side
        target = (xall.at[slot], ptsall.at[slot], packed.at[slot])[kind]
        other = jnp.minimum(me + 1, n - 1) if side == 0 else jnp.maximum(me - 1, 0)
        return pltpu.make_async_remote_copy(
            src_ref=sources[kind],
            dst_ref=target,
            send_sem=halo_send.at[kind, side],
            recv_sem=halo_recv.at[kind, side],
            device_id={"leaf": other},
            device_id_type=MESH,
        )

    def sends(side):
        return me < n - 1 if side == 0 else me > 0

    def receives(side):
        return me > 0 if side == 0 else me < n - 1

    for side in range(2):

        @pl.when(sends(side))
        def _():
            halo(0, side).start()
            halo(1, side).start()

    def up(node):
        return dot_nt(call[node], tr_ref[node])

    def keep(node, value):
        call[node] = value
        half = node % 2 * rank
        packed[1, node // 2, :, half : half + rank] = value

    for i in range(leaf_count):
        keep(i, dot_nt(x_ref[:, i * leaf : (i + 1) * leaf], basis_ref[i]))
    for height in range(1, len(counts) - 1):
        below = offsets[height - 1]
        for j in range(counts[height]):
            keep(offsets[height] + j, up(below + 2 * j) + up(below + 2 * j + 1))
    for side in range(2):

        @pl.when(sends(side))
        def _():
            halo(2, side).start()

    root = up(lower - 2) + up(lower - 1)
    roots[me] = jnp.zeros(roots.shape[1:], f32)
    roots[me, 0:vecs, 0:rank] = root
    roots[me, 0:vecs, rank : 2 * rank] = dot_nt(root, tr_ref[lower])
    roots[me, vecs : vecs + 2, 0:entries] = ulist_ref[...].astype(f32)

    def root_copy(d):
        return pltpu.make_async_remote_copy(
            src_ref=roots.at[me],
            dst_ref=roots.at[me],
            send_sem=root_send.at[d],
            recv_sem=root_recv.at[d],
            device_id={"leaf": lax.rem(me + d, n)},
            device_id_type=MESH,
        )

    def root_arrival(d):
        sender = lax.rem(me + n - d, n)
        return pltpu.make_async_remote_copy(
            src_ref=roots.at[me],
            dst_ref=roots.at[sender],
            send_sem=root_send.at[d],
            recv_sem=root_recv.at[d],
            device_id={"leaf": lax.rem(me + d, n)},
            device_id_type=MESH,
        )

    each(1, n, lambda d: root_copy(d).start())

    xall[1] = x_ref[...]
    ptsall[1] = pts_ref[:, 0:halo_width]
    for side in range(2):
        slot = 2 * side

        @pl.when(jnp.logical_not(receives(side)))
        def _():
            xall[slot] = jnp.zeros(xall.shape[1:], f32)
            ptsall[slot] = jnp.zeros(ptsall.shape[1:], f32)
            packed[slot] = jnp.zeros(packed.shape[1:], f32)

    total = nlist_ref.shape[1]
    row_hot = (
        lax.broadcasted_iota(jnp.int32, (leaf_count, total), 0) == nlist_ref[0:1, :]
    ).astype(f32).astype(bf16)
    col_hot = (
        lax.broadcasted_iota(jnp.int32, (128, total), 0) == nlist_ref[1:2, :]
    ).astype(f32).astype(bf16)
    count = lax.dot_general(
        row_hot, col_hot, (((1,), (1,)), ((), ())), preferred_element_type=f32
    )
    has = (count > 0.5).astype(f32)
    before = (
        lax.broadcasted_iota(jnp.int32, (128, 128), 0)
        < lax.broadcasted_iota(jnp.int32, (128, 128), 1)
    ).astype(f32).astype(bf16)
    place = dot_fast(has.astype(bf16), before)
    place = jnp.where(has > 0.5, place, -1.0)
    lane = lax.broadcasted_iota(jnp.int32, (leaf_count, 128), 1)
    lane_f = lane.astype(f32)
    cols = jnp.zeros((leaf_count, 128), f32)
    wts = jnp.zeros((leaf_count, 128), f32)
    for c in range(3 * leaf_count):
        hit = place[:, c : c + 1] == lane_f
        cols = cols + jnp.where(hit, float(c), 0.0)
        wts = wts + jnp.where(hit, count[:, c : c + 1], 0.0)
    filled = jnp.sum(has, axis=1, keepdims=True)
    cols_out[...] = jnp.where(lane == 127, filled, cols).astype(jnp.int32)
    wts_out[...] = wts * ln2

    for side in range(2):

        @pl.when(sends(side))
        def _():
            for kind in range(3):
                halo(kind, side).wait_send()

        @pl.when(receives(side))
        def _():
            for kind in range(3):
                halo(kind, side).wait_recv()

    def finish(d):
        root_copy(d).wait_send()
        root_arrival(d).wait_recv()

    each(1, n, finish)


def split(values):
    high = values.astype(bf16)
    return high, (values - high.astype(f32)).astype(bf16)


def kernel_values(squared):
    squared = jnp.maximum(squared, 1e-20)
    t = squared * lax.rsqrt(squared)
    return (t + log2e) * jnp.exp2(-t)


def product(values, kernel):
    kernel_high, kernel_low = split(kernel)
    high, low = split(values)
    rows = values.shape[0]
    both = dot_fast(jnp.concatenate([high, low], axis=0), kernel_high)
    return both[:rows] + both[rows:] + dot_fast(high, kernel_low)


def couple_kernel(
    n,
    entries,
    cols_ref,
    wts_ref,
    far_ref,
    xall,
    ptsall,
    uppts_ref,
    packed,
    roots,
    basis_ref,
    tr_ref,
    uptr_ref,
    out_ref,
    feat,
    near_t,
    near_row,
    skel_t,
    skel_row,
    up_t,
    up_row,
    y_ref,
    upc,
    call,
):
    me = lax.axis_index("leaf")
    leaf_count, rank, leaf = basis_ref.shape
    vecs = out_ref.shape[0]
    lower = 2 * leaf_count - 2
    npts = leaf_count * leaf
    nskel = lower * rank
    offsets, counts = level_table(leaf_count)
    up_offsets, up_counts = level_table(n)

    def features(p):
        q = (p - 0.5) * point_scale
        high = q.astype(bf16).astype(f32)
        low = (q - high).astype(bf16).astype(f32)
        q = high + low
        norm = jnp.sum(q * q, axis=0, keepdims=True)
        n1 = norm.astype(bf16).astype(f32)
        n2 = (norm - n1).astype(bf16).astype(f32)
        n3 = norm - n1 - n2
        return high, low, n1, n2, n3

    def put(p, width):
        high, low, n1, n2, n3 = features(p)
        span = slice(0, width)
        one = jnp.ones((1, width), f32)
        for k, rows in enumerate((high, low, high, low)):
            feat[0, 3 * k : 3 * k + 3, span] = -2.0 * rows
        for k, rows in enumerate((high, high, low, low)):
            feat[1, 3 * k : 3 * k + 3, span] = rows
        for k, rows in enumerate((n1, n2, n3, one, one, one)):
            feat[0, 12 + k : 13 + k, span] = rows
        for k, rows in enumerate((one, one, one, n1, n2, n3)):
            feat[1, 12 + k : 13 + k, span] = rows

    def columns_to(target, first, start, width):
        for t in range(width // 128):
            tile = feat[0, :, start + t * 128 : start + (t + 1) * 128]
            target[first + t * 128 : first + (t + 1) * 128, :] = tile.T.astype(bf16)

    feat[...] = jnp.zeros(feat.shape, f32)
    for slot in range(3):
        put(ptsall[slot], npts + nskel)
        columns_to(near_t, slot * npts, 0, npts)
        columns_to(skel_t, slot * nskel, npts, nskel)
        if slot == 1:
            near_row[...] = feat[1, :, 0:npts].astype(bf16)
            skel_row[...] = jnp.zeros(skel_row.shape, bf16)
            for j in range(lower):
                tile = feat[1, :, npts + j * rank : npts + (j + 1) * rank].astype(bf16)
                for h in range(2):
                    skel_row[2 * j + h, :, h * rank : (h + 1) * rank] = tile

    chunk = math.gcd(uppts_ref.shape[1], 1024)

    def up_chunk(i):
        base = i * chunk if isinstance(i, int) else pl.multiple_of(i * chunk, chunk)
        put(uppts_ref[:, pl.ds(base, chunk)], chunk)
        for t in range(chunk // 128):
            tile = feat[0, :, t * 128 : (t + 1) * 128]
            up_t[pl.ds(base + t * 128, 128), :] = tile.T.astype(bf16)
        for j in range(chunk // rank):
            up_row[i * (chunk // rank) + j] = feat[1, :, j * rank : (j + 1) * rank].astype(bf16)

    each(0, uppts_ref.shape[1] // chunk, up_chunk)

    def load_roots(j):
        upc[j] = roots[j, 0:vecs, 0:rank]

    each(0, n, load_roots)

    def first_lift(j):
        upc[n + j] = roots[2 * j, 0:vecs, rank : 2 * rank] + roots[2 * j + 1, 0:vecs, rank : 2 * rank]

    each(0, n // 2, first_lift)
    for height in range(2, len(up_counts)):

        def lift(j, height=height):
            child = up_offsets[height - 1] + 2 * j
            upc[up_offsets[height] + j] = dot_nt(upc[child], uptr_ref[child - n]) + dot_nt(
                upc[child + 1], uptr_ref[child + 1 - n]
            )

        each(0, up_counts[height], lift)

    pair_rows = roots[:, vecs, :]
    pair_cols = roots[:, vecs + 1, :]
    used = lax.broadcasted_iota(jnp.int32, pair_rows.shape, 1) < entries
    value = None
    for height in range(len(up_counts) - 1, -1, -1):
        node = up_offsets[height] + lax.div(me, 2**height)
        mine = jnp.logical_and(pair_rows == node.astype(f32), used)
        row_feat = up_row[node]

        def term(c, mine=mine, row_feat=row_feat):
            named = jnp.logical_and(mine, pair_cols == jnp.asarray(c, f32))
            times = jnp.sum(jnp.sum(jnp.where(named, ln2, 0.0), axis=1, keepdims=True), axis=0, keepdims=True)
            start = c * rank if isinstance(c, int) else pl.multiple_of(c * rank, rank)
            kernel = kernel_values(dot_fast(up_t[pl.ds(start, rank), :], row_feat))
            return product(upc[c] * times, kernel)

        first = up_offsets[height]
        if up_counts[height] <= 16:
            level = sum(term(first + j) for j in range(up_counts[height]))
        else:
            level = lax.fori_loop(
                0,
                up_counts[height],
                lambda j, acc: acc + term(first + j),
                jnp.zeros((vecs, rank), f32),
            )
        if value is not None:
            if height == 0:
                level = level + dot_nn(value, tr_ref[lower])
            else:
                level = level + dot_nn(value, uptr_ref[node - n])
        value = level

    y_ref[...] = jnp.zeros(y_ref.shape, f32)
    y_ref[lower] = value * (1.0 / ln2)

    for slot in range(3):
        for j in range(lower):
            half = j % 2 * rank
            call[slot * lower + j] = packed[slot, j // 2, :, half : half + rank]
    far_total = far_ref.shape[1]
    far_group = math.gcd(far_total, FAR_GROUP)

    @pl.loop(0, far_total // far_group)
    def _(g):
        named = [
            (far_ref[0, g * far_group + k], far_ref[1, g * far_group + k]) for k in range(far_group)
        ]
        tiles = []
        for k in range(0, far_group, 2):
            tiles.append(
                sum(
                    dot_fast(
                        skel_t[pl.ds(pl.multiple_of(named[k + h][1] * rank, rank), rank), :],
                        skel_row[2 * named[k + h][0] + h],
                    )
                    for h in range(2)
                )
            )
        kernel_high, kernel_low = split(kernel_values(jnp.concatenate(tiles, axis=0)))
        parts = []
        for k in range(0, far_group, 2):
            rows = slice(k // 2 * rank, (k // 2 + 1) * rank)
            high, low = split(
                jnp.concatenate([call[named[k][1]], call[named[k + 1][1]]], axis=0)
            )
            both = dot_fast(jnp.concatenate([high, low], axis=0), kernel_high[rows])
            parts.append(
                both[: 2 * vecs] + both[2 * vecs :] + dot_fast(high, kernel_low[rows])
            )
        for k in range(far_group):
            h = k % 2
            y_ref[named[k][0]] += parts[k // 2][h * vecs : (h + 1) * vecs, h * rank : (h + 1) * rank]

    for height in range(len(counts) - 2, -1, -1):
        for j in range(counts[height]):
            node = offsets[height] + j
            y_ref[node] += dot_nn(y_ref[offsets[height + 1] + j // 2], tr_ref[node])

    @pl.loop(0, leaf_count)
    def _(r):
        lanes = pl.ds(pl.multiple_of(r * leaf, leaf), leaf)
        row_feat = near_row[:, lanes]
        filled = cols_ref[r, 127]
        wide = lax.div(filled + (GROUP // 2 - 1), GROUP)
        narrow = lax.div(jnp.maximum(filled - wide * GROUP, 0) + (GROUP // 2 - 1), GROUP // 2)

        def near_group(first, size, acc):
            values = []
            places = []
            for k in range(size):
                c = cols_ref[r, first + k]
                slot = lax.div(c, leaf_count)
                inside = pl.multiple_of((c - slot * leaf_count) * leaf, leaf)
                values.append(xall[slot, :, pl.ds(inside, leaf)] * wts_ref[r, first + k])
                places.append(near_t[pl.ds(pl.multiple_of(c * leaf, leaf), leaf), :])
            kernel = kernel_values(dot_fast(jnp.concatenate(places, axis=0), row_feat))
            return acc + product(jnp.concatenate(values, axis=1), kernel)

        acc = lax.fori_loop(
            0, wide, lambda g, acc: near_group(g * GROUP, GROUP, acc), jnp.zeros((vecs, leaf), f32)
        )
        acc = lax.fori_loop(
            0, narrow, lambda g, acc: near_group(wide * GROUP, GROUP // 2, acc), acc
        )
        out_ref[:, lanes] = acc + dot_nn(y_ref[r] * ln2, basis_ref[r])


def per_device(
    vectors,
    points,
    leaf_basis,
    local_transfer,
    local_skeleton,
    upper_transfer,
    upper_skeleton,
    near_list,
    far_list,
    upper_list,
):
    leaf_count, rank, leaf = leaf_basis.shape
    vecs, npts = vectors.shape
    n = lax.axis_size("leaf")
    lower = 2 * leaf_count - 2
    nskel = lower * rank
    halo_width = npts + nskel
    nup = 2 * n * rank
    vmem = pl.BlockSpec(memory_space=pltpu.VMEM)
    smem = pl.BlockSpec(memory_space=pltpu.SMEM)
    pts = jnp.concatenate(
        [points, jnp.transpose(local_skeleton, (1, 0, 2)).reshape(3, nskel)], axis=1
    )
    uppts = jnp.pad(
        jnp.transpose(upper_skeleton, (1, 0, 2)).reshape(3, (2 * n - 1) * rank), ((0, 0), (0, rank))
    )
    root_rows = vecs + 8
    xall, ptsall, packed, roots, cols, wts = pl.pallas_call(
        functools.partial(exchange_kernel, n, halo_width),
        out_shape=(
            jax.ShapeDtypeStruct((3, vecs, npts), f32),
            jax.ShapeDtypeStruct((3, 3, halo_width), f32),
            jax.ShapeDtypeStruct((3, lower // 2, vecs, 2 * rank), f32),
            jax.ShapeDtypeStruct((n, root_rows, 2 * rank), f32),
            jax.ShapeDtypeStruct((leaf_count, 128), jnp.int32),
            jax.ShapeDtypeStruct((leaf_count, 128), f32),
        ),
        in_specs=[vmem] * 6,
        out_specs=(vmem,) * 6,
        scratch_shapes=[
            pltpu.SemaphoreType.DMA((3, 2)),
            pltpu.SemaphoreType.DMA((3, 2)),
            pltpu.SemaphoreType.DMA((n,)),
            pltpu.SemaphoreType.DMA((n,)),
            pltpu.VMEM((lower, vecs, rank), f32),
        ],
        compiler_params=pltpu.CompilerParams(
            collective_id=0, has_side_effects=True, vmem_limit_bytes=40 * 2**20
        ),
    )(vectors, pts, leaf_basis, local_transfer, upper_list, near_list)
    return pl.pallas_call(
        functools.partial(couple_kernel, n, upper_list.shape[1]),
        out_shape=jax.ShapeDtypeStruct((vecs, npts), f32),
        in_specs=[smem] * 3 + [vmem] * 8,
        out_specs=vmem,
        scratch_shapes=[
            pltpu.VMEM((2, FEATURES, halo_width), f32),
            pltpu.VMEM((3 * npts, FEATURES), bf16),
            pltpu.VMEM((FEATURES, npts), bf16),
            pltpu.VMEM((3 * nskel, FEATURES), bf16),
            pltpu.VMEM((2 * lower, FEATURES, 2 * rank), bf16),
            pltpu.VMEM((nup, FEATURES), bf16),
            pltpu.VMEM((2 * n, FEATURES, rank), bf16),
            pltpu.VMEM((lower + 1, vecs, rank), f32),
            pltpu.VMEM((2 * n, vecs, rank), f32),
            pltpu.VMEM((3 * lower, vecs, rank), f32),
        ],
        compiler_params=pltpu.CompilerParams(vmem_limit_bytes=48 * 2**20),
    )(cols, wts, far_list, xall, ptsall, uppts, packed, roots, leaf_basis, local_transfer, upper_transfer)


def solution(mesh):
    return jax.shard_map(
        per_device,
        mesh=mesh,
        in_specs=(
            P("sub", ("groups", "leaf")),
            P(None, ("groups", "leaf")),
            P(("groups", "leaf"), None, None),
            P(("groups", "leaf"), None, None),
            P(("groups", "leaf"), None, None),
            P(),
            P(),
            P(None, ("groups", "leaf")),
            P(None, ("groups", "leaf")),
            P(None, ("groups", "leaf")),
        ),
        out_specs=P("sub", ("groups", "leaf")),
        check_vma=False,
    )
```

```python
import functools
import math

import jax
import jax.numpy as jnp
from jax import lax
from jax.experimental import pallas as pl
from jax.experimental.pallas import tpu as pltpu
from jax.sharding import PartitionSpec as P

root_three = math.sqrt(3.0)
length_scale = 0.3
log2e = math.log2(math.e)
ln2 = math.log(2.0)
point_scale = root_three / length_scale * log2e
highest = lax.Precision.HIGHEST
MESH = pl.DeviceIdType.MESH
FEATURES = 32
GROUP = 16
FAR_GROUP = 16
f32 = jnp.float32
bf16 = jnp.bfloat16


def level_table(count):
    offsets = []
    counts = []
    anchor = 0
    extent = count
    while extent >= 1:
        offsets.append(anchor)
        counts.append(extent)
        anchor += extent
        extent //= 2
    return (offsets, counts)


def dot_nt(a, b):
    return lax.dot_general(
        a, b, (((1,), (1,)), ((), ())), precision=highest, preferred_element_type=f32
    )


def dot_nn(a, b):
    return lax.dot_general(
        a, b, (((1,), (0,)), ((), ())), precision=highest, preferred_element_type=f32
    )


def dot_fast(a, b):
    return lax.dot_general(a, b, (((1,), (0,)), ((), ())), preferred_element_type=f32)


def each(start, stop, body):
    if stop - start <= 16:
        for i in range(start, stop):
            body(i)
    else:

        @pl.loop(start, stop)
        def _(i):
            body(i)


def split(values):
    high = values.astype(bf16)
    return high, (values - high.astype(f32)).astype(bf16)


def kernel_values(squared):
    squared = jnp.maximum(squared, 1e-20)
    t = squared * lax.rsqrt(squared)
    return (t + log2e) * jnp.exp2(-t)


def product(values, kernel):
    kernel_high, kernel_low = split(kernel)
    high, low = split(values)
    rows = values.shape[0]
    both = dot_fast(jnp.concatenate([high, low], axis=0), kernel_high)
    return both[:rows] + both[rows:] + dot_fast(high, kernel_low)


def features(p):
    q = (p - 0.5) * point_scale
    high = q.astype(bf16).astype(f32)
    low = (q - high).astype(bf16).astype(f32)
    q = high + low
    norm = jnp.sum(q * q, axis=0, keepdims=True)
    n1 = norm.astype(bf16).astype(f32)
    n2 = (norm - n1).astype(bf16).astype(f32)
    n3 = norm - n1 - n2
    return high, low, n1, n2, n3


def put_features(feat, p, width):
    high, low, n1, n2, n3 = features(p)
    span = slice(0, width)
    one = jnp.ones((1, width), f32)
    for k, rows in enumerate((high, low, high, low)):
        feat[0, 3 * k : 3 * k + 3, span] = -2.0 * rows
    for k, rows in enumerate((high, high, low, low)):
        feat[1, 3 * k : 3 * k + 3, span] = rows
    for k, rows in enumerate((n1, n2, n3, one, one, one)):
        feat[0, 12 + k : 13 + k, span] = rows
    for k, rows in enumerate((one, one, one, n1, n2, n3)):
        feat[1, 12 + k : 13 + k, span] = rows


def exchange_kernel(
    n,
    halo_width,
    x_ref,
    pts_ref,
    basis_ref,
    tr_ref,
    ulist_ref,
    nlist_ref,
    xall,
    ptsall,
    packed,
    roots,
    cols_out,
    wts_out,
    own_out,
    halo_send,
    halo_recv,
    root_send,
    root_recv,
    call,
    feat,
    near_t,
    near_row,
    spread,
):
    me = lax.axis_index("leaf")
    leaf_count, rank, leaf = basis_ref.shape
    vecs = x_ref.shape[0]
    lower = 2 * leaf_count - 2
    offsets, counts = level_table(leaf_count)
    entries = ulist_ref.shape[1]

    barrier = pltpu.get_barrier_semaphore()

    def greet(d):
        pl.semaphore_signal(
            barrier, inc=1, device_id={"leaf": lax.rem(me + d, n)}, device_id_type=MESH
        )

    each(1, n, greet)
    pl.semaphore_wait(barrier, n - 1)

    own_pts = pts_ref.at[:, pl.ds(0, halo_width)]
    own_coefs = packed.at[1]
    sources = (x_ref, own_pts, own_coefs)

    def halo(kind, side):
        slot = 2 * side
        target = (xall.at[slot], ptsall.at[slot], packed.at[slot])[kind]
        other = jnp.minimum(me + 1, n - 1) if side == 0 else jnp.maximum(me - 1, 0)
        return pltpu.make_async_remote_copy(
            src_ref=sources[kind],
            dst_ref=target,
            send_sem=halo_send.at[kind, side],
            recv_sem=halo_recv.at[kind, side],
            device_id={"leaf": other},
            device_id_type=MESH,
        )

    def sends(side):
        return me < n - 1 if side == 0 else me > 0

    def receives(side):
        return me > 0 if side == 0 else me < n - 1

    for side in range(2):

        @pl.when(sends(side))
        def _():
            halo(0, side).start()
            halo(1, side).start()

    def up(node):
        return dot_nt(call[node], tr_ref[node])

    def keep(node, value):
        call[node] = value
        half = node % 2 * rank
        packed[1, node // 2, :, half : half + rank] = value

    for i in range(leaf_count):
        keep(i, dot_nt(x_ref[:, i * leaf : (i + 1) * leaf], basis_ref[i]))
    for height in range(1, len(counts) - 1):
        below = offsets[height - 1]
        for j in range(counts[height]):
            keep(offsets[height] + j, up(below + 2 * j) + up(below + 2 * j + 1))
    for side in range(2):

        @pl.when(sends(side))
        def _():
            halo(2, side).start()

    root = up(lower - 2) + up(lower - 1)
    roots[me] = jnp.zeros(roots.shape[1:], f32)
    roots[me, 0:vecs, 0:rank] = root
    roots[me, 0:vecs, rank : 2 * rank] = dot_nt(root, tr_ref[lower])
    roots[me, vecs : vecs + 2, 0:entries] = ulist_ref[...].astype(f32)

    def root_copy(d):
        return pltpu.make_async_remote_copy(
            src_ref=roots.at[me],
            dst_ref=roots.at[me],
            send_sem=root_send.at[d],
            recv_sem=root_recv.at[d],
            device_id={"leaf": lax.rem(me + d, n)},
            device_id_type=MESH,
        )

    def root_arrival(d):
        sender = lax.rem(me + n - d, n)
        return pltpu.make_async_remote_copy(
            src_ref=roots.at[me],
            dst_ref=roots.at[sender],
            send_sem=root_send.at[d],
            recv_sem=root_recv.at[d],
            device_id={"leaf": lax.rem(me + d, n)},
            device_id_type=MESH,
        )

    each(1, n, lambda d: root_copy(d).start())

    xall[1] = x_ref[...]
    ptsall[1] = pts_ref[:, 0:halo_width]
    for side in range(2):
        slot = 2 * side

        @pl.when(jnp.logical_not(receives(side)))
        def _():
            xall[slot] = jnp.zeros(xall.shape[1:], f32)
            ptsall[slot] = jnp.zeros(ptsall.shape[1:], f32)
            packed[slot] = jnp.zeros(packed.shape[1:], f32)

    total = nlist_ref.shape[1]
    row_hot = (
        lax.broadcasted_iota(jnp.int32, (leaf_count, total), 0) == nlist_ref[0:1, :]
    ).astype(f32).astype(bf16)
    col_hot = (
        lax.broadcasted_iota(jnp.int32, (128, total), 0) == nlist_ref[1:2, :]
    ).astype(f32).astype(bf16)
    count = lax.dot_general(
        row_hot, col_hot, (((1,), (1,)), ((), ())), preferred_element_type=f32
    )
    col_id = lax.broadcasted_iota(jnp.int32, count.shape, 1)
    own = jnp.logical_and(col_id >= leaf_count, col_id < 2 * leaf_count)
    has = jnp.where(jnp.logical_or(own, count < 0.5), 0.0, 1.0)
    before = (
        lax.broadcasted_iota(jnp.int32, (128, 128), 0)
        < lax.broadcasted_iota(jnp.int32, (128, 128), 1)
    ).astype(f32).astype(bf16)
    place = dot_fast(has.astype(bf16), before)
    place = jnp.where(has > 0.5, place, -1.0)
    lane = lax.broadcasted_iota(jnp.int32, (leaf_count, 128), 1)
    lane_f = lane.astype(f32)
    cols = jnp.zeros((leaf_count, 128), f32)
    wts = jnp.zeros((leaf_count, 128), f32)
    for c in [*range(leaf_count), *range(2 * leaf_count, 3 * leaf_count)]:
        hit = place[:, c : c + 1] == lane_f
        cols = cols + jnp.where(hit, float(c), 0.0)
        wts = wts + jnp.where(hit, count[:, c : c + 1], 0.0)
    filled = jnp.sum(has, axis=1, keepdims=True)
    cols_out[...] = jnp.where(lane == 127, filled, cols).astype(jnp.int32)
    wts_out[...] = wts * ln2

    npts = leaf_count * leaf
    put_features(feat, pts_ref[:, 0:npts], npts)
    feat[:, 18:FEATURES, :] = jnp.zeros((2, FEATURES - 18, npts), f32)
    near_row[...] = feat[1].astype(bf16)
    for i in range(leaf_count):
        near_t[i * leaf : (i + 1) * leaf, :] = feat[0, :, i * leaf : (i + 1) * leaf].T.astype(bf16)
    leaf_of = lax.broadcasted_iota(jnp.int32, (128, npts), 1) // leaf + leaf_count
    chosen = (leaf_of == lax.broadcasted_iota(jnp.int32, (128, npts), 0)).astype(f32)
    spread[...] = dot_nn(count * ln2, chosen)

    @pl.loop(0, leaf_count)
    def _(r):
        lanes = pl.ds(pl.multiple_of(r * leaf, leaf), leaf)
        kernel = kernel_values(dot_fast(near_t[...], near_row[:, lanes]))
        own_out[:, lanes] = product(x_ref[...] * spread[pl.ds(r, 1), :], kernel)

    for side in range(2):

        @pl.when(sends(side))
        def _():
            for kind in range(3):
                halo(kind, side).wait_send()

        @pl.when(receives(side))
        def _():
            for kind in range(3):
                halo(kind, side).wait_recv()

    def finish(d):
        root_copy(d).wait_send()
        root_arrival(d).wait_recv()

    each(1, n, finish)


def couple_kernel(
    n,
    entries,
    cols_ref,
    wts_ref,
    far_ref,
    xall,
    ptsall,
    uppts_ref,
    packed,
    roots,
    basis_ref,
    tr_ref,
    uptr_ref,
    own_ref,
    out_ref,
    feat,
    near_t,
    near_row,
    skel_t,
    skel_row,
    up_t,
    up_row,
    y_ref,
    upc,
    call,
):
    me = lax.axis_index("leaf")
    leaf_count, rank, leaf = basis_ref.shape
    vecs = out_ref.shape[0]
    lower = 2 * leaf_count - 2
    npts = leaf_count * leaf
    nskel = lower * rank
    offsets, counts = level_table(leaf_count)
    up_offsets, up_counts = level_table(n)

    put = functools.partial(put_features, feat)

    def columns_to(target, first, start, width):
        for t in range(width // 128):
            tile = feat[0, :, start + t * 128 : start + (t + 1) * 128]
            target[first + t * 128 : first + (t + 1) * 128, :] = tile.T.astype(bf16)

    feat[...] = jnp.zeros(feat.shape, f32)
    for slot in range(3):
        put(ptsall[slot], npts + nskel)
        columns_to(near_t, slot * npts, 0, npts)
        columns_to(skel_t, slot * nskel, npts, nskel)
        if slot == 1:
            near_row[...] = feat[1, :, 0:npts].astype(bf16)
            skel_row[...] = jnp.zeros(skel_row.shape, bf16)
            for j in range(lower):
                tile = feat[1, :, npts + j * rank : npts + (j + 1) * rank].astype(bf16)
                for h in range(2):
                    skel_row[2 * j + h, :, h * rank : (h + 1) * rank] = tile

    chunk = math.gcd(uppts_ref.shape[1], 1024)

    def up_chunk(i):
        base = i * chunk if isinstance(i, int) else pl.multiple_of(i * chunk, chunk)
        put(uppts_ref[:, pl.ds(base, chunk)], chunk)
        for t in range(chunk // 128):
            tile = feat[0, :, t * 128 : (t + 1) * 128]
            up_t[pl.ds(base + t * 128, 128), :] = tile.T.astype(bf16)
        for j in range(chunk // rank):
            up_row[i * (chunk // rank) + j] = feat[1, :, j * rank : (j + 1) * rank].astype(bf16)

    each(0, uppts_ref.shape[1] // chunk, up_chunk)

    def load_roots(j):
        upc[j] = roots[j, 0:vecs, 0:rank]

    each(0, n, load_roots)

    def first_lift(j):
        upc[n + j] = roots[2 * j, 0:vecs, rank : 2 * rank] + roots[2 * j + 1, 0:vecs, rank : 2 * rank]

    each(0, n // 2, first_lift)
    for height in range(2, len(up_counts)):

        def lift(j, height=height):
            child = up_offsets[height - 1] + 2 * j
            upc[up_offsets[height] + j] = dot_nt(upc[child], uptr_ref[child - n]) + dot_nt(
                upc[child + 1], uptr_ref[child + 1 - n]
            )

        each(0, up_counts[height], lift)

    pair_rows = roots[:, vecs, :]
    pair_cols = roots[:, vecs + 1, :]
    used = lax.broadcasted_iota(jnp.int32, pair_rows.shape, 1) < entries
    value = None
    for height in range(len(up_counts) - 1, -1, -1):
        node = up_offsets[height] + lax.div(me, 2**height)
        mine = jnp.logical_and(pair_rows == node.astype(f32), used)
        row_feat = up_row[node]

        def term(c, mine=mine, row_feat=row_feat):
            named = jnp.logical_and(mine, pair_cols == jnp.asarray(c, f32))
            times = jnp.sum(jnp.sum(jnp.where(named, ln2, 0.0), axis=1, keepdims=True), axis=0, keepdims=True)
            start = c * rank if isinstance(c, int) else pl.multiple_of(c * rank, rank)
            kernel = kernel_values(dot_fast(up_t[pl.ds(start, rank), :], row_feat))
            return product(upc[c] * times, kernel)

        first = up_offsets[height]
        if up_counts[height] <= 16:
            level = sum(term(first + j) for j in range(up_counts[height]))
        else:
            level = lax.fori_loop(
                0,
                up_counts[height],
                lambda j, acc: acc + term(first + j),
                jnp.zeros((vecs, rank), f32),
            )
        if value is not None:
            if height == 0:
                level = level + dot_nn(value, tr_ref[lower])
            else:
                level = level + dot_nn(value, uptr_ref[node - n])
        value = level

    y_ref[...] = jnp.zeros(y_ref.shape, f32)
    y_ref[lower] = value * (1.0 / ln2)

    for slot in range(3):
        for j in range(lower):
            half = j % 2 * rank
            call[slot * lower + j] = packed[slot, j // 2, :, half : half + rank]
    far_total = far_ref.shape[1]
    far_group = math.gcd(far_total, FAR_GROUP)

    @pl.loop(0, far_total // far_group)
    def _(g):
        named = [
            (far_ref[0, g * far_group + k], far_ref[1, g * far_group + k]) for k in range(far_group)
        ]
        tiles = []
        for k in range(0, far_group, 2):
            tiles.append(
                sum(
                    dot_fast(
                        skel_t[pl.ds(pl.multiple_of(named[k + h][1] * rank, rank), rank), :],
                        skel_row[2 * named[k + h][0] + h],
                    )
                    for h in range(2)
                )
            )
        kernel_high, kernel_low = split(kernel_values(jnp.concatenate(tiles, axis=0)))
        parts = []
        for k in range(0, far_group, 2):
            rows = slice(k // 2 * rank, (k // 2 + 1) * rank)
            high, low = split(
                jnp.concatenate([call[named[k][1]], call[named[k + 1][1]]], axis=0)
            )
            both = dot_fast(jnp.concatenate([high, low], axis=0), kernel_high[rows])
            parts.append(
                both[: 2 * vecs] + both[2 * vecs :] + dot_fast(high, kernel_low[rows])
            )
        for k in range(far_group):
            h = k % 2
            y_ref[named[k][0]] += parts[k // 2][h * vecs : (h + 1) * vecs, h * rank : (h + 1) * rank]

    for height in range(len(counts) - 2, -1, -1):
        for j in range(counts[height]):
            node = offsets[height] + j
            y_ref[node] += dot_nn(y_ref[offsets[height + 1] + j // 2], tr_ref[node])

    @pl.loop(0, leaf_count)
    def _(r):
        lanes = pl.ds(pl.multiple_of(r * leaf, leaf), leaf)
        row_feat = near_row[:, lanes]
        filled = cols_ref[r, 127]
        wide = lax.div(filled + (GROUP // 2 - 1), GROUP)
        narrow = lax.div(jnp.maximum(filled - wide * GROUP, 0) + (GROUP // 2 - 1), GROUP // 2)

        def near_group(first, size, acc):
            values = []
            places = []
            for k in range(size):
                c = cols_ref[r, first + k]
                slot = lax.div(c, leaf_count)
                inside = pl.multiple_of((c - slot * leaf_count) * leaf, leaf)
                values.append(xall[slot, :, pl.ds(inside, leaf)] * wts_ref[r, first + k])
                places.append(near_t[pl.ds(pl.multiple_of(c * leaf, leaf), leaf), :])
            kernel = kernel_values(dot_fast(jnp.concatenate(places, axis=0), row_feat))
            return acc + product(jnp.concatenate(values, axis=1), kernel)

        acc = lax.fori_loop(
            0, wide, lambda g, acc: near_group(g * GROUP, GROUP, acc), own_ref[:, lanes]
        )
        acc = lax.fori_loop(
            0, narrow, lambda g, acc: near_group(wide * GROUP, GROUP // 2, acc), acc
        )
        out_ref[:, lanes] = acc + dot_nn(y_ref[r] * ln2, basis_ref[r])


def per_device(
    vectors,
    points,
    leaf_basis,
    local_transfer,
    local_skeleton,
    upper_transfer,
    upper_skeleton,
    near_list,
    far_list,
    upper_list,
):
    leaf_count, rank, leaf = leaf_basis.shape
    vecs, npts = vectors.shape
    n = lax.axis_size("leaf")
    lower = 2 * leaf_count - 2
    nskel = lower * rank
    halo_width = npts + nskel
    nup = 2 * n * rank
    vmem = pl.BlockSpec(memory_space=pltpu.VMEM)
    smem = pl.BlockSpec(memory_space=pltpu.SMEM)
    pts = jnp.concatenate(
        [points, jnp.transpose(local_skeleton, (1, 0, 2)).reshape(3, nskel)], axis=1
    )
    uppts = jnp.pad(
        jnp.transpose(upper_skeleton, (1, 0, 2)).reshape(3, (2 * n - 1) * rank), ((0, 0), (0, rank))
    )
    root_rows = vecs + 8
    xall, ptsall, packed, roots, cols, wts, near_own = pl.pallas_call(
        functools.partial(exchange_kernel, n, halo_width),
        out_shape=(
            jax.ShapeDtypeStruct((3, vecs, npts), f32),
            jax.ShapeDtypeStruct((3, 3, halo_width), f32),
            jax.ShapeDtypeStruct((3, lower // 2, vecs, 2 * rank), f32),
            jax.ShapeDtypeStruct((n, root_rows, 2 * rank), f32),
            jax.ShapeDtypeStruct((leaf_count, 128), jnp.int32),
            jax.ShapeDtypeStruct((leaf_count, 128), f32),
            jax.ShapeDtypeStruct((vecs, npts), f32),
        ),
        in_specs=[vmem] * 6,
        out_specs=(vmem,) * 7,
        scratch_shapes=[
            pltpu.SemaphoreType.DMA((3, 2)),
            pltpu.SemaphoreType.DMA((3, 2)),
            pltpu.SemaphoreType.DMA((n,)),
            pltpu.SemaphoreType.DMA((n,)),
            pltpu.VMEM((lower, vecs, rank), f32),
            pltpu.VMEM((2, FEATURES, npts), f32),
            pltpu.VMEM((npts, FEATURES), bf16),
            pltpu.VMEM((FEATURES, npts), bf16),
            pltpu.VMEM((leaf_count, npts), f32),
        ],
        compiler_params=pltpu.CompilerParams(
            collective_id=0, has_side_effects=True, vmem_limit_bytes=40 * 2**20
        ),
    )(vectors, pts, leaf_basis, local_transfer, upper_list, near_list)
    return pl.pallas_call(
        functools.partial(couple_kernel, n, upper_list.shape[1]),
        out_shape=jax.ShapeDtypeStruct((vecs, npts), f32),
        in_specs=[smem] * 3 + [vmem] * 9,
        out_specs=vmem,
        scratch_shapes=[
            pltpu.VMEM((2, FEATURES, halo_width), f32),
            pltpu.VMEM((3 * npts, FEATURES), bf16),
            pltpu.VMEM((FEATURES, npts), bf16),
            pltpu.VMEM((3 * nskel, FEATURES), bf16),
            pltpu.VMEM((2 * lower, FEATURES, 2 * rank), bf16),
            pltpu.VMEM((nup, FEATURES), bf16),
            pltpu.VMEM((2 * n, FEATURES, rank), bf16),
            pltpu.VMEM((lower + 1, vecs, rank), f32),
            pltpu.VMEM((2 * n, vecs, rank), f32),
            pltpu.VMEM((3 * lower, vecs, rank), f32),
        ],
        compiler_params=pltpu.CompilerParams(vmem_limit_bytes=48 * 2**20),
    )(cols, wts, far_list, xall, ptsall, uppts, packed, roots, leaf_basis, local_transfer, upper_transfer, near_own)


def solution(mesh):
    return jax.shard_map(
        per_device,
        mesh=mesh,
        in_specs=(
            P("sub", ("groups", "leaf")),
            P(None, ("groups", "leaf")),
            P(("groups", "leaf"), None, None),
            P(("groups", "leaf"), None, None),
            P(("groups", "leaf"), None, None),
            P(),
            P(),
            P(None, ("groups", "leaf")),
            P(None, ("groups", "leaf")),
            P(None, ("groups", "leaf")),
        ),
        out_specs=P("sub", ("groups", "leaf")),
        check_vma=False,
    )
```

```python
import functools
import math

import jax
import jax.numpy as jnp
from jax import lax
from jax.experimental import pallas as pl
from jax.experimental.pallas import tpu as pltpu
from jax.sharding import PartitionSpec as P

root_three = math.sqrt(3.0)
length_scale = 0.3
log2e = math.log2(math.e)
ln2 = math.log(2.0)
point_scale = root_three / length_scale * log2e
highest = lax.Precision.HIGHEST
MESH = pl.DeviceIdType.MESH
FEATURES = 32
GROUP = 16
FAR_GROUP = 16
f32 = jnp.float32
bf16 = jnp.bfloat16


def level_table(count):
    offsets = []
    counts = []
    anchor = 0
    extent = count
    while extent >= 1:
        offsets.append(anchor)
        counts.append(extent)
        anchor += extent
        extent //= 2
    return (offsets, counts)


def dot_nt(a, b):
    return lax.dot_general(
        a, b, (((1,), (1,)), ((), ())), precision=highest, preferred_element_type=f32
    )


def dot_nn(a, b):
    return lax.dot_general(
        a, b, (((1,), (0,)), ((), ())), precision=highest, preferred_element_type=f32
    )


def dot_fast(a, b):
    return lax.dot_general(a, b, (((1,), (0,)), ((), ())), preferred_element_type=f32)


def each(start, stop, body):
    if stop - start <= 16:
        for i in range(start, stop):
            body(i)
    else:

        @pl.loop(start, stop)
        def _(i):
            body(i)


def split(values):
    high = values.astype(bf16)
    return high, (values - high.astype(f32)).astype(bf16)


def kernel_values(squared):
    squared = jnp.maximum(squared, 1e-20)
    t = squared * lax.rsqrt(squared)
    return (t + log2e) * jnp.exp2(-t)


def product(values, kernel):
    kernel_high, kernel_low = split(kernel)
    high, low = split(values)
    rows = values.shape[0]
    both = dot_fast(jnp.concatenate([high, low], axis=0), kernel_high)
    return both[:rows] + both[rows:] + dot_fast(high, kernel_low)


def features(p):
    q = (p - 0.5) * point_scale
    high = q.astype(bf16).astype(f32)
    low = (q - high).astype(bf16).astype(f32)
    q = high + low
    norm = jnp.sum(q * q, axis=0, keepdims=True)
    n1 = norm.astype(bf16).astype(f32)
    n2 = (norm - n1).astype(bf16).astype(f32)
    n3 = norm - n1 - n2
    return high, low, n1, n2, n3


def put_features(feat, p, width):
    high, low, n1, n2, n3 = features(p)
    span = slice(0, width)
    one = jnp.ones((1, width), f32)
    for k, rows in enumerate((high, low, high, low)):
        feat[0, 3 * k : 3 * k + 3, span] = -2.0 * rows
    for k, rows in enumerate((high, high, low, low)):
        feat[1, 3 * k : 3 * k + 3, span] = rows
    for k, rows in enumerate((n1, n2, n3, one, one, one)):
        feat[0, 12 + k : 13 + k, span] = rows
    for k, rows in enumerate((one, one, one, n1, n2, n3)):
        feat[1, 12 + k : 13 + k, span] = rows


def exchange_kernel(
    n,
    halo_width,
    x_ref,
    pts_ref,
    basis_ref,
    tr_ref,
    ulist_ref,
    nlist_ref,
    xall,
    ptsall,
    packed,
    roots,
    cols_out,
    wts_out,
    own_out,
    halo_send,
    halo_recv,
    root_send,
    root_recv,
    call,
    feat,
    near_t,
    near_row,
    spread,
):
    me = lax.axis_index("leaf")
    leaf_count, rank, leaf = basis_ref.shape
    vecs = x_ref.shape[0]
    lower = 2 * leaf_count - 2
    offsets, counts = level_table(leaf_count)
    entries = ulist_ref.shape[1]

    barrier = pltpu.get_barrier_semaphore()

    def greet(d):
        pl.semaphore_signal(
            barrier, inc=1, device_id={"leaf": lax.rem(me + d, n)}, device_id_type=MESH
        )

    each(1, n, greet)
    pl.semaphore_wait(barrier, n - 1)

    own_pts = pts_ref.at[:, pl.ds(0, halo_width)]
    own_coefs = packed.at[1]
    sources = (x_ref, own_pts, own_coefs)

    def halo(kind, side):
        slot = 2 * side
        target = (xall.at[slot], ptsall.at[slot], packed.at[slot])[kind]
        other = jnp.minimum(me + 1, n - 1) if side == 0 else jnp.maximum(me - 1, 0)
        return pltpu.make_async_remote_copy(
            src_ref=sources[kind],
            dst_ref=target,
            send_sem=halo_send.at[kind, side],
            recv_sem=halo_recv.at[kind, side],
            device_id={"leaf": other},
            device_id_type=MESH,
        )

    def sends(side):
        return me < n - 1 if side == 0 else me > 0

    def receives(side):
        return me > 0 if side == 0 else me < n - 1

    for side in range(2):

        @pl.when(sends(side))
        def _():
            halo(0, side).start()
            halo(1, side).start()

    def up(node):
        return dot_nt(call[node], tr_ref[node])

    def keep(node, value):
        call[node] = value
        half = node % 2 * rank
        packed[1, node // 2, :, half : half + rank] = value

    for i in range(leaf_count):
        keep(i, dot_nt(x_ref[:, i * leaf : (i + 1) * leaf], basis_ref[i]))
    for height in range(1, len(counts) - 1):
        below = offsets[height - 1]
        for j in range(counts[height]):
            keep(offsets[height] + j, up(below + 2 * j) + up(below + 2 * j + 1))
    for side in range(2):

        @pl.when(sends(side))
        def _():
            halo(2, side).start()

    root = up(lower - 2) + up(lower - 1)
    roots[me] = jnp.zeros(roots.shape[1:], f32)
    roots[me, 0:vecs, 0:rank] = root
    roots[me, 0:vecs, rank : 2 * rank] = dot_nt(root, tr_ref[lower])
    roots[me, vecs : vecs + 2, 0:entries] = ulist_ref[...].astype(f32)

    def root_copy(d):
        return pltpu.make_async_remote_copy(
            src_ref=roots.at[me],
            dst_ref=roots.at[me],
            send_sem=root_send.at[d],
            recv_sem=root_recv.at[d],
            device_id={"leaf": lax.rem(me + d, n)},
            device_id_type=MESH,
        )

    def root_arrival(d):
        sender = lax.rem(me + n - d, n)
        return pltpu.make_async_remote_copy(
            src_ref=roots.at[me],
            dst_ref=roots.at[sender],
            send_sem=root_send.at[d],
            recv_sem=root_recv.at[d],
            device_id={"leaf": lax.rem(me + d, n)},
            device_id_type=MESH,
        )

    each(1, n, lambda d: root_copy(d).start())

    xall[1] = x_ref[...]
    ptsall[1] = pts_ref[:, 0:halo_width]
    for side in range(2):
        slot = 2 * side

        @pl.when(jnp.logical_not(receives(side)))
        def _():
            xall[slot] = jnp.zeros(xall.shape[1:], f32)
            ptsall[slot] = jnp.zeros(ptsall.shape[1:], f32)
            packed[slot] = jnp.zeros(packed.shape[1:], f32)

    total = nlist_ref.shape[1]
    row_hot = (
        lax.broadcasted_iota(jnp.int32, (leaf_count, total), 0) == nlist_ref[0:1, :]
    ).astype(f32).astype(bf16)
    col_hot = (
        lax.broadcasted_iota(jnp.int32, (128, total), 0) == nlist_ref[1:2, :]
    ).astype(f32).astype(bf16)
    count = lax.dot_general(
        row_hot, col_hot, (((1,), (1,)), ((), ())), preferred_element_type=f32
    )
    col_id = lax.broadcasted_iota(jnp.int32, count.shape, 1)
    own = jnp.logical_and(col_id >= leaf_count, col_id < 2 * leaf_count)
    has = jnp.where(jnp.logical_or(own, count < 0.5), 0.0, 1.0)
    before = (
        lax.broadcasted_iota(jnp.int32, (128, 128), 0)
        < lax.broadcasted_iota(jnp.int32, (128, 128), 1)
    ).astype(f32).astype(bf16)
    place = dot_fast(has.astype(bf16), before)
    place = jnp.where(has > 0.5, place, -1.0)
    lane = lax.broadcasted_iota(jnp.int32, (leaf_count, 128), 1)
    lane_f = lane.astype(f32)
    cols = jnp.zeros((leaf_count, 128), f32)
    wts = jnp.zeros((leaf_count, 128), f32)
    for c in [*range(leaf_count), *range(2 * leaf_count, 3 * leaf_count)]:
        hit = place[:, c : c + 1] == lane_f
        cols = cols + jnp.where(hit, float(c), 0.0)
        wts = wts + jnp.where(hit, count[:, c : c + 1], 0.0)
    filled = jnp.sum(has, axis=1, keepdims=True)
    cols_out[...] = jnp.where(lane == 127, filled, cols).astype(jnp.int32)
    wts_out[...] = wts * ln2

    npts = leaf_count * leaf
    put_features(feat, pts_ref[:, 0:npts], npts)
    feat[:, 18:FEATURES, :] = jnp.zeros((2, FEATURES - 18, npts), f32)
    near_row[...] = feat[1].astype(bf16)
    for i in range(leaf_count):
        near_t[i * leaf : (i + 1) * leaf, :] = feat[0, :, i * leaf : (i + 1) * leaf].T.astype(bf16)
    leaf_of = lax.broadcasted_iota(jnp.int32, (128, npts), 1) // leaf + leaf_count
    chosen = (leaf_of == lax.broadcasted_iota(jnp.int32, (128, npts), 0)).astype(f32)
    spread[...] = dot_nn(count * ln2, chosen)

    @pl.loop(0, leaf_count)
    def _(r):
        lanes = pl.ds(pl.multiple_of(r * leaf, leaf), leaf)
        kernel = kernel_values(dot_fast(near_t[...], near_row[:, lanes]))
        own_out[:, lanes] = product(x_ref[...] * spread[pl.ds(r, 1), :], kernel)

    for side in range(2):

        @pl.when(sends(side))
        def _():
            for kind in range(3):
                halo(kind, side).wait_send()

        @pl.when(receives(side))
        def _():
            for kind in range(3):
                halo(kind, side).wait_recv()

    def finish(d):
        root_copy(d).wait_send()
        root_arrival(d).wait_recv()

    each(1, n, finish)


def couple_kernel(
    n,
    entries,
    cols_ref,
    wts_ref,
    far_ref,
    xall,
    ptsall,
    uppts_ref,
    packed,
    roots,
    basis_ref,
    tr_ref,
    uptr_ref,
    own_ref,
    out_ref,
    feat,
    near_t,
    near_row,
    skel_t,
    skel_row,
    up_t,
    up_row,
    y_ref,
    upc,
    call,
):
    me = lax.axis_index("leaf")
    leaf_count, rank, leaf = basis_ref.shape
    vecs = out_ref.shape[0]
    lower = 2 * leaf_count - 2
    npts = leaf_count * leaf
    nskel = lower * rank
    offsets, counts = level_table(leaf_count)
    up_offsets, up_counts = level_table(n)

    put = functools.partial(put_features, feat)

    def columns_to(target, first, start, width):
        for t in range(width // 128):
            tile = feat[0, :, start + t * 128 : start + (t + 1) * 128]
            target[first + t * 128 : first + (t + 1) * 128, :] = tile.T.astype(bf16)

    feat[...] = jnp.zeros(feat.shape, f32)
    for slot in range(3):
        put(ptsall[slot], npts + nskel)
        columns_to(near_t, slot * npts, 0, npts)
        columns_to(skel_t, slot * nskel, npts, nskel)
        if slot == 1:
            near_row[...] = feat[1, :, 0:npts].astype(bf16)
            skel_row[...] = jnp.zeros(skel_row.shape, bf16)
            for j in range(lower):
                tile = feat[1, :, npts + j * rank : npts + (j + 1) * rank].astype(bf16)
                for h in range(2):
                    skel_row[2 * j + h, :, h * rank : (h + 1) * rank] = tile

    chunk = math.gcd(uppts_ref.shape[1], 1024)

    def up_chunk(i):
        base = i * chunk if isinstance(i, int) else pl.multiple_of(i * chunk, chunk)
        put(uppts_ref[:, pl.ds(base, chunk)], chunk)
        for t in range(chunk // 128):
            tile = feat[0, :, t * 128 : (t + 1) * 128]
            up_t[pl.ds(base + t * 128, 128), :] = tile.T.astype(bf16)
        for j in range(chunk // rank):
            up_row[i * (chunk // rank) + j] = feat[1, :, j * rank : (j + 1) * rank].astype(bf16)

    each(0, uppts_ref.shape[1] // chunk, up_chunk)

    def load_roots(j):
        upc[j] = roots[j, 0:vecs, 0:rank]

    each(0, n, load_roots)

    def first_lift(j):
        upc[n + j] = roots[2 * j, 0:vecs, rank : 2 * rank] + roots[2 * j + 1, 0:vecs, rank : 2 * rank]

    each(0, n // 2, first_lift)
    for height in range(2, len(up_counts)):

        def lift(j, height=height):
            child = up_offsets[height - 1] + 2 * j
            upc[up_offsets[height] + j] = dot_nt(upc[child], uptr_ref[child - n]) + dot_nt(
                upc[child + 1], uptr_ref[child + 1 - n]
            )

        each(0, up_counts[height], lift)

    pair_rows = roots[:, vecs, :]
    pair_cols = roots[:, vecs + 1, :]
    used = lax.broadcasted_iota(jnp.int32, pair_rows.shape, 1) < entries
    value = None
    for height in range(len(up_counts) - 1, -1, -1):
        node = up_offsets[height] + lax.div(me, 2**height)
        mine = jnp.logical_and(pair_rows == node.astype(f32), used)
        row_feat = up_row[node]

        def term(c, mine=mine, row_feat=row_feat):
            named = jnp.logical_and(mine, pair_cols == jnp.asarray(c, f32))
            times = jnp.sum(jnp.sum(jnp.where(named, ln2, 0.0), axis=1, keepdims=True), axis=0, keepdims=True)
            start = c * rank if isinstance(c, int) else pl.multiple_of(c * rank, rank)
            kernel = kernel_values(dot_fast(up_t[pl.ds(start, rank), :], row_feat))
            return product(upc[c] * times, kernel)

        first = up_offsets[height]
        if up_counts[height] <= 16:
            level = sum(term(first + j) for j in range(up_counts[height]))
        else:
            level = lax.fori_loop(
                0,
                up_counts[height],
                lambda j, acc: acc + term(first + j),
                jnp.zeros((vecs, rank), f32),
            )
        if value is not None:
            if height == 0:
                level = level + dot_nn(value, tr_ref[lower])
            else:
                level = level + dot_nn(value, uptr_ref[node - n])
        value = level

    y_ref[...] = jnp.zeros(y_ref.shape, f32)
    y_ref[lower] = value * (1.0 / ln2)

    for slot in range(3):
        for j in range(lower):
            half = j % 2 * rank
            call[slot * lower + j] = packed[slot, j // 2, :, half : half + rank]
    far_total = far_ref.shape[1]
    far_group = math.gcd(far_total, FAR_GROUP)

    @pl.loop(0, far_total // far_group)
    def _(g):
        named = [
            (far_ref[0, g * far_group + k], far_ref[1, g * far_group + k]) for k in range(far_group)
        ]
        tiles = []
        for k in range(0, far_group, 2):
            tiles.append(
                sum(
                    dot_fast(
                        skel_t[pl.ds(pl.multiple_of(named[k + h][1] * rank, rank), rank), :],
                        skel_row[2 * named[k + h][0] + h],
                    )
                    for h in range(2)
                )
            )
        kernel_high, kernel_low = split(kernel_values(jnp.concatenate(tiles, axis=0)))
        parts = []
        for k in range(0, far_group, 2):
            rows = slice(k // 2 * rank, (k // 2 + 1) * rank)
            high, low = split(
                jnp.concatenate([call[named[k][1]], call[named[k + 1][1]]], axis=0)
            )
            both = dot_fast(jnp.concatenate([high, low], axis=0), kernel_high[rows])
            parts.append(
                both[: 2 * vecs] + both[2 * vecs :] + dot_fast(high, kernel_low[rows])
            )
        for k in range(far_group):
            h = k % 2
            y_ref[named[k][0]] += parts[k // 2][h * vecs : (h + 1) * vecs, h * rank : (h + 1) * rank]

    for height in range(len(counts) - 2, -1, -1):
        for j in range(counts[height]):
            node = offsets[height] + j
            y_ref[node] += dot_nn(y_ref[offsets[height + 1] + j // 2], tr_ref[node])

    for i in range(leaf_count):
        span = slice(i * leaf, (i + 1) * leaf)
        out_ref[:, span] = own_ref[:, span] + dot_nn(y_ref[i] * ln2, basis_ref[i])

    @pl.loop(0, leaf_count)
    def _(r):
        lanes = pl.ds(pl.multiple_of(r * leaf, leaf), leaf)
        row_feat = near_row[:, lanes]
        filled = cols_ref[r, 127]
        wide = lax.div(filled + (GROUP // 2 - 1), GROUP)
        narrow = lax.div(jnp.maximum(filled - wide * GROUP, 0) + (GROUP // 2 - 1), GROUP // 2)

        def near_group(first, size, acc):
            values = []
            places = []
            for k in range(size):
                c = cols_ref[r, first + k]
                slot = lax.div(c, leaf_count)
                inside = pl.multiple_of((c - slot * leaf_count) * leaf, leaf)
                values.append(xall[slot, :, pl.ds(inside, leaf)] * wts_ref[r, first + k])
                places.append(near_t[pl.ds(pl.multiple_of(c * leaf, leaf), leaf), :])
            kernel = kernel_values(dot_fast(jnp.concatenate(places, axis=0), row_feat))
            return acc + product(jnp.concatenate(values, axis=1), kernel)

        acc = lax.fori_loop(
            0, wide, lambda g, acc: near_group(g * GROUP, GROUP, acc), out_ref[:, lanes]
        )
        acc = lax.fori_loop(
            0, narrow, lambda g, acc: near_group(wide * GROUP, GROUP // 2, acc), acc
        )
        out_ref[:, lanes] = acc


def per_device(
    vectors,
    points,
    leaf_basis,
    local_transfer,
    local_skeleton,
    upper_transfer,
    upper_skeleton,
    near_list,
    far_list,
    upper_list,
):
    leaf_count, rank, leaf = leaf_basis.shape
    vecs, npts = vectors.shape
    n = lax.axis_size("leaf")
    lower = 2 * leaf_count - 2
    nskel = lower * rank
    halo_width = npts + nskel
    nup = 2 * n * rank
    vmem = pl.BlockSpec(memory_space=pltpu.VMEM)
    smem = pl.BlockSpec(memory_space=pltpu.SMEM)
    pts = jnp.concatenate(
        [points, jnp.transpose(local_skeleton, (1, 0, 2)).reshape(3, nskel)], axis=1
    )
    uppts = jnp.pad(
        jnp.transpose(upper_skeleton, (1, 0, 2)).reshape(3, (2 * n - 1) * rank), ((0, 0), (0, rank))
    )
    root_rows = vecs + 8
    xall, ptsall, packed, roots, cols, wts, near_own = pl.pallas_call(
        functools.partial(exchange_kernel, n, halo_width),
        out_shape=(
            jax.ShapeDtypeStruct((3, vecs, npts), f32),
            jax.ShapeDtypeStruct((3, 3, halo_width), f32),
            jax.ShapeDtypeStruct((3, lower // 2, vecs, 2 * rank), f32),
            jax.ShapeDtypeStruct((n, root_rows, 2 * rank), f32),
            jax.ShapeDtypeStruct((leaf_count, 128), jnp.int32),
            jax.ShapeDtypeStruct((leaf_count, 128), f32),
            jax.ShapeDtypeStruct((vecs, npts), f32),
        ),
        in_specs=[vmem] * 6,
        out_specs=(vmem,) * 7,
        scratch_shapes=[
            pltpu.SemaphoreType.DMA((3, 2)),
            pltpu.SemaphoreType.DMA((3, 2)),
            pltpu.SemaphoreType.DMA((n,)),
            pltpu.SemaphoreType.DMA((n,)),
            pltpu.VMEM((lower, vecs, rank), f32),
            pltpu.VMEM((2, FEATURES, npts), f32),
            pltpu.VMEM((npts, FEATURES), bf16),
            pltpu.VMEM((FEATURES, npts), bf16),
            pltpu.VMEM((leaf_count, npts), f32),
        ],
        compiler_params=pltpu.CompilerParams(
            collective_id=0, has_side_effects=True, vmem_limit_bytes=40 * 2**20
        ),
    )(vectors, pts, leaf_basis, local_transfer, upper_list, near_list)
    return pl.pallas_call(
        functools.partial(couple_kernel, n, upper_list.shape[1]),
        out_shape=jax.ShapeDtypeStruct((vecs, npts), f32),
        in_specs=[smem] * 3 + [vmem] * 9,
        out_specs=vmem,
        scratch_shapes=[
            pltpu.VMEM((2, FEATURES, halo_width), f32),
            pltpu.VMEM((3 * npts, FEATURES), bf16),
            pltpu.VMEM((FEATURES, npts), bf16),
            pltpu.VMEM((3 * nskel, FEATURES), bf16),
            pltpu.VMEM((2 * lower, FEATURES, 2 * rank), bf16),
            pltpu.VMEM((nup, FEATURES), bf16),
            pltpu.VMEM((2 * n, FEATURES, rank), bf16),
            pltpu.VMEM((lower + 1, vecs, rank), f32),
            pltpu.VMEM((2 * n, vecs, rank), f32),
            pltpu.VMEM((3 * lower, vecs, rank), f32),
        ],
        compiler_params=pltpu.CompilerParams(vmem_limit_bytes=48 * 2**20),
    )(cols, wts, far_list, xall, ptsall, uppts, packed, roots, leaf_basis, local_transfer, upper_transfer, near_own)


def solution(mesh):
    return jax.shard_map(
        per_device,
        mesh=mesh,
        in_specs=(
            P("sub", ("groups", "leaf")),
            P(None, ("groups", "leaf")),
            P(("groups", "leaf"), None, None),
            P(("groups", "leaf"), None, None),
            P(("groups", "leaf"), None, None),
            P(),
            P(),
            P(None, ("groups", "leaf")),
            P(None, ("groups", "leaf")),
            P(None, ("groups", "leaf")),
        ),
        out_specs=P("sub", ("groups", "leaf")),
        check_vma=False,
    )
```

```python
import functools
import math

import jax
import jax.numpy as jnp
from jax import lax
from jax.experimental import pallas as pl
from jax.experimental.pallas import tpu as pltpu
from jax.sharding import PartitionSpec as P

root_three = math.sqrt(3.0)
length_scale = 0.3
log2e = math.log2(math.e)
ln2 = math.log(2.0)
point_scale = root_three / length_scale * log2e
highest = lax.Precision.HIGHEST
MESH = pl.DeviceIdType.MESH
FEATURES = 32
GROUP = 16
FAR_GROUP = 32
f32 = jnp.float32
bf16 = jnp.bfloat16


def level_table(count):
    offsets = []
    counts = []
    anchor = 0
    extent = count
    while extent >= 1:
        offsets.append(anchor)
        counts.append(extent)
        anchor += extent
        extent //= 2
    return (offsets, counts)


def dot_nt(a, b):
    return lax.dot_general(
        a, b, (((1,), (1,)), ((), ())), precision=highest, preferred_element_type=f32
    )


def dot_nn(a, b):
    return lax.dot_general(
        a, b, (((1,), (0,)), ((), ())), precision=highest, preferred_element_type=f32
    )


def dot_fast(a, b):
    return lax.dot_general(a, b, (((1,), (0,)), ((), ())), preferred_element_type=f32)


def each(start, stop, body):
    if stop - start <= 16:
        for i in range(start, stop):
            body(i)
    else:

        @pl.loop(start, stop)
        def _(i):
            body(i)


def split(values):
    high = values.astype(bf16)
    return high, (values - high.astype(f32)).astype(bf16)


def kernel_values(squared):
    squared = jnp.maximum(squared, 1e-20)
    t = squared * lax.rsqrt(squared)
    return (t + log2e) * jnp.exp2(-t)


def product(values, kernel):
    kernel_high, kernel_low = split(kernel)
    high, low = split(values)
    rows = values.shape[0]
    both = dot_fast(jnp.concatenate([high, low], axis=0), kernel_high)
    return both[:rows] + both[rows:] + dot_fast(high, kernel_low)


def features(p):
    q = (p - 0.5) * point_scale
    high = q.astype(bf16).astype(f32)
    low = (q - high).astype(bf16).astype(f32)
    q = high + low
    norm = jnp.sum(q * q, axis=0, keepdims=True)
    n1 = norm.astype(bf16).astype(f32)
    n2 = (norm - n1).astype(bf16).astype(f32)
    n3 = norm - n1 - n2
    return high, low, n1, n2, n3


def put_features(feat, p, width):
    high, low, n1, n2, n3 = features(p)
    span = slice(0, width)
    one = jnp.ones((1, width), f32)
    for k, rows in enumerate((high, low, high, low)):
        feat[0, 3 * k : 3 * k + 3, span] = -2.0 * rows
    for k, rows in enumerate((high, high, low, low)):
        feat[1, 3 * k : 3 * k + 3, span] = rows
    for k, rows in enumerate((n1, n2, n3, one, one, one)):
        feat[0, 12 + k : 13 + k, span] = rows
    for k, rows in enumerate((one, one, one, n1, n2, n3)):
        feat[1, 12 + k : 13 + k, span] = rows


def exchange_kernel(
    n,
    halo_width,
    x_ref,
    pts_ref,
    basis_ref,
    tr_ref,
    ulist_ref,
    nlist_ref,
    xall,
    ptsall,
    packed,
    roots,
    cols_out,
    wts_out,
    own_out,
    halo_send,
    halo_recv,
    root_send,
    root_recv,
    call,
    feat,
    near_t,
    near_row,
    spread,
):
    me = lax.axis_index("leaf")
    leaf_count, rank, leaf = basis_ref.shape
    vecs = x_ref.shape[0]
    lower = 2 * leaf_count - 2
    offsets, counts = level_table(leaf_count)
    entries = ulist_ref.shape[1]

    barrier = pltpu.get_barrier_semaphore()

    def greet(d):
        pl.semaphore_signal(
            barrier, inc=1, device_id={"leaf": lax.rem(me + d, n)}, device_id_type=MESH
        )

    each(1, n, greet)
    pl.semaphore_wait(barrier, n - 1)

    own_pts = pts_ref.at[:, pl.ds(0, halo_width)]
    own_coefs = packed.at[1]
    sources = (x_ref, own_pts, own_coefs)

    def halo(kind, side):
        slot = 2 * side
        target = (xall.at[slot], ptsall.at[slot], packed.at[slot])[kind]
        other = jnp.minimum(me + 1, n - 1) if side == 0 else jnp.maximum(me - 1, 0)
        return pltpu.make_async_remote_copy(
            src_ref=sources[kind],
            dst_ref=target,
            send_sem=halo_send.at[kind, side],
            recv_sem=halo_recv.at[kind, side],
            device_id={"leaf": other},
            device_id_type=MESH,
        )

    def sends(side):
        return me < n - 1 if side == 0 else me > 0

    def receives(side):
        return me > 0 if side == 0 else me < n - 1

    for side in range(2):

        @pl.when(sends(side))
        def _():
            halo(0, side).start()
            halo(1, side).start()

    def up(node):
        return dot_nt(call[node], tr_ref[node])

    def keep(node, value):
        call[node] = value
        half = node % 2 * rank
        packed[1, node // 2, :, half : half + rank] = value

    for i in range(leaf_count):
        keep(i, dot_nt(x_ref[:, i * leaf : (i + 1) * leaf], basis_ref[i]))
    for height in range(1, len(counts) - 1):
        below = offsets[height - 1]
        for j in range(counts[height]):
            keep(offsets[height] + j, up(below + 2 * j) + up(below + 2 * j + 1))
    for side in range(2):

        @pl.when(sends(side))
        def _():
            halo(2, side).start()

    root = up(lower - 2) + up(lower - 1)
    roots[me] = jnp.zeros(roots.shape[1:], f32)
    roots[me, 0:vecs, 0:rank] = root
    roots[me, 0:vecs, rank : 2 * rank] = dot_nt(root, tr_ref[lower])
    roots[me, vecs : vecs + 2, 0:entries] = ulist_ref[...].astype(f32)

    def root_copy(d):
        return pltpu.make_async_remote_copy(
            src_ref=roots.at[me],
            dst_ref=roots.at[me],
            send_sem=root_send.at[d],
            recv_sem=root_recv.at[d],
            device_id={"leaf": lax.rem(me + d, n)},
            device_id_type=MESH,
        )

    def root_arrival(d):
        sender = lax.rem(me + n - d, n)
        return pltpu.make_async_remote_copy(
            src_ref=roots.at[me],
            dst_ref=roots.at[sender],
            send_sem=root_send.at[d],
            recv_sem=root_recv.at[d],
            device_id={"leaf": lax.rem(me + d, n)},
            device_id_type=MESH,
        )

    each(1, n, lambda d: root_copy(d).start())

    xall[1] = x_ref[...]
    ptsall[1] = pts_ref[:, 0:halo_width]
    for side in range(2):
        slot = 2 * side

        @pl.when(jnp.logical_not(receives(side)))
        def _():
            xall[slot] = jnp.zeros(xall.shape[1:], f32)
            ptsall[slot] = jnp.zeros(ptsall.shape[1:], f32)
            packed[slot] = jnp.zeros(packed.shape[1:], f32)

    total = nlist_ref.shape[1]
    row_hot = (
        lax.broadcasted_iota(jnp.int32, (leaf_count, total), 0) == nlist_ref[0:1, :]
    ).astype(f32).astype(bf16)
    col_hot = (
        lax.broadcasted_iota(jnp.int32, (128, total), 0) == nlist_ref[1:2, :]
    ).astype(f32).astype(bf16)
    count = lax.dot_general(
        row_hot, col_hot, (((1,), (1,)), ((), ())), preferred_element_type=f32
    )
    col_id = lax.broadcasted_iota(jnp.int32, count.shape, 1)
    own = jnp.logical_and(col_id >= leaf_count, col_id < 2 * leaf_count)
    has = jnp.where(jnp.logical_or(own, count < 0.5), 0.0, 1.0)
    before = (
        lax.broadcasted_iota(jnp.int32, (128, 128), 0)
        < lax.broadcasted_iota(jnp.int32, (128, 128), 1)
    ).astype(f32).astype(bf16)
    place = dot_fast(has.astype(bf16), before)
    place = jnp.where(has > 0.5, place, -1.0)
    lane = lax.broadcasted_iota(jnp.int32, (leaf_count, 128), 1)
    lane_f = lane.astype(f32)
    cols = jnp.zeros((leaf_count, 128), f32)
    wts = jnp.zeros((leaf_count, 128), f32)
    for c in [*range(leaf_count), *range(2 * leaf_count, 3 * leaf_count)]:
        hit = place[:, c : c + 1] == lane_f
        cols = cols + jnp.where(hit, float(c), 0.0)
        wts = wts + jnp.where(hit, count[:, c : c + 1], 0.0)
    filled = jnp.sum(has, axis=1, keepdims=True)
    cols_out[...] = jnp.where(lane == 127, filled, cols).astype(jnp.int32)
    wts_out[...] = wts * ln2

    npts = leaf_count * leaf
    put_features(feat, pts_ref[:, 0:npts], npts)
    feat[:, 18:FEATURES, :] = jnp.zeros((2, FEATURES - 18, npts), f32)
    near_row[...] = feat[1].astype(bf16)
    for i in range(leaf_count):
        near_t[i * leaf : (i + 1) * leaf, :] = feat[0, :, i * leaf : (i + 1) * leaf].T.astype(bf16)
    leaf_of = lax.broadcasted_iota(jnp.int32, (128, npts), 1) // leaf + leaf_count
    chosen = (leaf_of == lax.broadcasted_iota(jnp.int32, (128, npts), 0)).astype(f32)
    spread[...] = dot_nn(count * ln2, chosen)

    @pl.loop(0, leaf_count)
    def _(r):
        lanes = pl.ds(pl.multiple_of(r * leaf, leaf), leaf)
        kernel = kernel_values(dot_fast(near_t[...], near_row[:, lanes]))
        own_out[:, lanes] = product(x_ref[...] * spread[pl.ds(r, 1), :], kernel)

    for side in range(2):

        @pl.when(sends(side))
        def _():
            for kind in range(3):
                halo(kind, side).wait_send()

        @pl.when(receives(side))
        def _():
            for kind in range(3):
                halo(kind, side).wait_recv()

    def finish(d):
        root_copy(d).wait_send()
        root_arrival(d).wait_recv()

    each(1, n, finish)


def couple_kernel(
    n,
    entries,
    cols_ref,
    wts_ref,
    far_ref,
    xall,
    ptsall,
    uppts_ref,
    packed,
    roots,
    basis_ref,
    tr_ref,
    uptr_ref,
    own_ref,
    out_ref,
    feat,
    near_t,
    near_row,
    skel_t,
    skel_row,
    up_t,
    up_row,
    y_ref,
    upc,
    call,
):
    me = lax.axis_index("leaf")
    leaf_count, rank, leaf = basis_ref.shape
    vecs = out_ref.shape[0]
    lower = 2 * leaf_count - 2
    npts = leaf_count * leaf
    nskel = lower * rank
    offsets, counts = level_table(leaf_count)
    up_offsets, up_counts = level_table(n)

    put = functools.partial(put_features, feat)

    def columns_to(target, first, start, width):
        for t in range(width // 128):
            tile = feat[0, :, start + t * 128 : start + (t + 1) * 128]
            target[first + t * 128 : first + (t + 1) * 128, :] = tile.T.astype(bf16)

    feat[...] = jnp.zeros(feat.shape, f32)
    for slot in range(3):
        put(ptsall[slot], npts + nskel)
        columns_to(near_t, slot * npts, 0, npts)
        columns_to(skel_t, slot * nskel, npts, nskel)
        if slot == 1:
            near_row[...] = feat[1, :, 0:npts].astype(bf16)
            skel_row[...] = jnp.zeros(skel_row.shape, bf16)
            for j in range(lower):
                tile = feat[1, :, npts + j * rank : npts + (j + 1) * rank].astype(bf16)
                for h in range(2):
                    skel_row[2 * j + h, :, h * rank : (h + 1) * rank] = tile

    chunk = math.gcd(uppts_ref.shape[1], 1024)

    def up_chunk(i):
        base = i * chunk if isinstance(i, int) else pl.multiple_of(i * chunk, chunk)
        put(uppts_ref[:, pl.ds(base, chunk)], chunk)
        for t in range(chunk // 128):
            tile = feat[0, :, t * 128 : (t + 1) * 128]
            up_t[pl.ds(base + t * 128, 128), :] = tile.T.astype(bf16)
        for j in range(chunk // rank):
            up_row[i * (chunk // rank) + j] = feat[1, :, j * rank : (j + 1) * rank].astype(bf16)

    each(0, uppts_ref.shape[1] // chunk, up_chunk)

    def load_roots(j):
        upc[j] = roots[j, 0:vecs, 0:rank]

    each(0, n, load_roots)

    def first_lift(j):
        upc[n + j] = roots[2 * j, 0:vecs, rank : 2 * rank] + roots[2 * j + 1, 0:vecs, rank : 2 * rank]

    each(0, n // 2, first_lift)
    for height in range(2, len(up_counts)):

        def lift(j, height=height):
            child = up_offsets[height - 1] + 2 * j
            upc[up_offsets[height] + j] = dot_nt(upc[child], uptr_ref[child - n]) + dot_nt(
                upc[child + 1], uptr_ref[child + 1 - n]
            )

        each(0, up_counts[height], lift)

    pair_rows = roots[:, vecs, :]
    pair_cols = roots[:, vecs + 1, :]
    used = lax.broadcasted_iota(jnp.int32, pair_rows.shape, 1) < entries
    value = None
    for height in range(len(up_counts) - 1, -1, -1):
        node = up_offsets[height] + lax.div(me, 2**height)
        mine = jnp.logical_and(pair_rows == node.astype(f32), used)
        row_feat = up_row[node]

        def term(c, mine=mine, row_feat=row_feat):
            named = jnp.logical_and(mine, pair_cols == jnp.asarray(c, f32))
            times = jnp.sum(jnp.sum(jnp.where(named, ln2, 0.0), axis=1, keepdims=True), axis=0, keepdims=True)
            start = c * rank if isinstance(c, int) else pl.multiple_of(c * rank, rank)
            kernel = kernel_values(dot_fast(up_t[pl.ds(start, rank), :], row_feat))
            return product(upc[c] * times, kernel)

        first = up_offsets[height]
        if up_counts[height] <= 16:
            level = sum(term(first + j) for j in range(up_counts[height]))
        else:
            level = lax.fori_loop(
                0,
                up_counts[height],
                lambda j, acc: acc + term(first + j),
                jnp.zeros((vecs, rank), f32),
            )
        if value is not None:
            if height == 0:
                level = level + dot_nn(value, tr_ref[lower])
            else:
                level = level + dot_nn(value, uptr_ref[node - n])
        value = level

    y_ref[...] = jnp.zeros(y_ref.shape, f32)
    y_ref[lower] = value * (1.0 / ln2)

    for slot in range(3):
        for j in range(lower):
            half = j % 2 * rank
            call[slot * lower + j] = packed[slot, j // 2, :, half : half + rank]
    far_total = far_ref.shape[1]
    far_group = math.gcd(far_total, FAR_GROUP)

    @pl.loop(0, far_total // far_group)
    def _(g):
        named = [
            (far_ref[0, g * far_group + k], far_ref[1, g * far_group + k]) for k in range(far_group)
        ]
        tiles = []
        for k in range(0, far_group, 2):
            tiles.append(
                sum(
                    dot_fast(
                        skel_t[pl.ds(pl.multiple_of(named[k + h][1] * rank, rank), rank), :],
                        skel_row[2 * named[k + h][0] + h],
                    )
                    for h in range(2)
                )
            )
        kernel_high, kernel_low = split(kernel_values(jnp.concatenate(tiles, axis=0)))
        parts = []
        for k in range(0, far_group, 2):
            rows = slice(k // 2 * rank, (k // 2 + 1) * rank)
            high, low = split(
                jnp.concatenate([call[named[k][1]], call[named[k + 1][1]]], axis=0)
            )
            both = dot_fast(jnp.concatenate([high, low], axis=0), kernel_high[rows])
            parts.append(
                both[: 2 * vecs] + both[2 * vecs :] + dot_fast(high, kernel_low[rows])
            )
        for k in range(far_group):
            h = k % 2
            y_ref[named[k][0]] += parts[k // 2][h * vecs : (h + 1) * vecs, h * rank : (h + 1) * rank]

    for height in range(len(counts) - 2, -1, -1):
        for j in range(counts[height]):
            node = offsets[height] + j
            y_ref[node] += dot_nn(y_ref[offsets[height + 1] + j // 2], tr_ref[node])

    for i in range(leaf_count):
        span = slice(i * leaf, (i + 1) * leaf)
        out_ref[:, span] = own_ref[:, span] + dot_nn(y_ref[i] * ln2, basis_ref[i])

    @pl.loop(0, leaf_count)
    def _(r):
        lanes = pl.ds(pl.multiple_of(r * leaf, leaf), leaf)
        row_feat = near_row[:, lanes]
        filled = cols_ref[r, 127]
        wide = lax.div(filled + (GROUP // 2 - 1), GROUP)
        narrow = lax.div(jnp.maximum(filled - wide * GROUP, 0) + (GROUP // 2 - 1), GROUP // 2)

        def near_group(first, size, acc):
            values = []
            places = []
            for k in range(size):
                c = cols_ref[r, first + k]
                slot = lax.div(c, leaf_count)
                inside = pl.multiple_of((c - slot * leaf_count) * leaf, leaf)
                values.append(xall[slot, :, pl.ds(inside, leaf)] * wts_ref[r, first + k])
                places.append(near_t[pl.ds(pl.multiple_of(c * leaf, leaf), leaf), :])
            kernel = kernel_values(dot_fast(jnp.concatenate(places, axis=0), row_feat))
            return acc + product(jnp.concatenate(values, axis=1), kernel)

        acc = lax.fori_loop(
            0, wide, lambda g, acc: near_group(g * GROUP, GROUP, acc), out_ref[:, lanes]
        )
        acc = lax.fori_loop(
            0, narrow, lambda g, acc: near_group(wide * GROUP, GROUP // 2, acc), acc
        )
        out_ref[:, lanes] = acc


def per_device(
    vectors,
    points,
    leaf_basis,
    local_transfer,
    local_skeleton,
    upper_transfer,
    upper_skeleton,
    near_list,
    far_list,
    upper_list,
):
    leaf_count, rank, leaf = leaf_basis.shape
    vecs, npts = vectors.shape
    n = lax.axis_size("leaf")
    lower = 2 * leaf_count - 2
    nskel = lower * rank
    halo_width = npts + nskel
    nup = 2 * n * rank
    vmem = pl.BlockSpec(memory_space=pltpu.VMEM)
    smem = pl.BlockSpec(memory_space=pltpu.SMEM)
    pts = jnp.concatenate(
        [points, jnp.transpose(local_skeleton, (1, 0, 2)).reshape(3, nskel)], axis=1
    )
    uppts = jnp.pad(
        jnp.transpose(upper_skeleton, (1, 0, 2)).reshape(3, (2 * n - 1) * rank), ((0, 0), (0, rank))
    )
    root_rows = vecs + 8
    xall, ptsall, packed, roots, cols, wts, near_own = pl.pallas_call(
        functools.partial(exchange_kernel, n, halo_width),
        out_shape=(
            jax.ShapeDtypeStruct((3, vecs, npts), f32),
            jax.ShapeDtypeStruct((3, 3, halo_width), f32),
            jax.ShapeDtypeStruct((3, lower // 2, vecs, 2 * rank), f32),
            jax.ShapeDtypeStruct((n, root_rows, 2 * rank), f32),
            jax.ShapeDtypeStruct((leaf_count, 128), jnp.int32),
            jax.ShapeDtypeStruct((leaf_count, 128), f32),
            jax.ShapeDtypeStruct((vecs, npts), f32),
        ),
        in_specs=[vmem] * 6,
        out_specs=(vmem,) * 7,
        scratch_shapes=[
            pltpu.SemaphoreType.DMA((3, 2)),
            pltpu.SemaphoreType.DMA((3, 2)),
            pltpu.SemaphoreType.DMA((n,)),
            pltpu.SemaphoreType.DMA((n,)),
            pltpu.VMEM((lower, vecs, rank), f32),
            pltpu.VMEM((2, FEATURES, npts), f32),
            pltpu.VMEM((npts, FEATURES), bf16),
            pltpu.VMEM((FEATURES, npts), bf16),
            pltpu.VMEM((leaf_count, npts), f32),
        ],
        compiler_params=pltpu.CompilerParams(
            collective_id=0, has_side_effects=True, vmem_limit_bytes=40 * 2**20
        ),
    )(vectors, pts, leaf_basis, local_transfer, upper_list, near_list)
    return pl.pallas_call(
        functools.partial(couple_kernel, n, upper_list.shape[1]),
        out_shape=jax.ShapeDtypeStruct((vecs, npts), f32),
        in_specs=[smem] * 3 + [vmem] * 9,
        out_specs=vmem,
        scratch_shapes=[
            pltpu.VMEM((2, FEATURES, halo_width), f32),
            pltpu.VMEM((3 * npts, FEATURES), bf16),
            pltpu.VMEM((FEATURES, npts), bf16),
            pltpu.VMEM((3 * nskel, FEATURES), bf16),
            pltpu.VMEM((2 * lower, FEATURES, 2 * rank), bf16),
            pltpu.VMEM((nup, FEATURES), bf16),
            pltpu.VMEM((2 * n, FEATURES, rank), bf16),
            pltpu.VMEM((lower + 1, vecs, rank), f32),
            pltpu.VMEM((2 * n, vecs, rank), f32),
            pltpu.VMEM((3 * lower, vecs, rank), f32),
        ],
        compiler_params=pltpu.CompilerParams(vmem_limit_bytes=48 * 2**20),
    )(cols, wts, far_list, xall, ptsall, uppts, packed, roots, leaf_basis, local_transfer, upper_transfer, near_own)


def solution(mesh):
    return jax.shard_map(
        per_device,
        mesh=mesh,
        in_specs=(
            P("sub", ("groups", "leaf")),
            P(None, ("groups", "leaf")),
            P(("groups", "leaf"), None, None),
            P(("groups", "leaf"), None, None),
            P(("groups", "leaf"), None, None),
            P(),
            P(),
            P(None, ("groups", "leaf")),
            P(None, ("groups", "leaf")),
            P(None, ("groups", "leaf")),
        ),
        out_specs=P("sub", ("groups", "leaf")),
        check_vma=False,
    )
```
